256 devices in a mesh: tensor: 32 (over x, z), dp: 8 (over y, core).
Axes of the slice: x: 4, y: 4, z: 8, core: 2. Of those that a mesh axis runs over, the one named last changes fastest.
Arguments:
- inputs: bfloat16 [256, 128, 28672], P('dp', None, 'tensor'), may hold values from -6 to 6
- out_grads: bfloat16 [256, 128, 8192], P('dp', None, 'tensor'), may hold values from -6 to 6
- proj_in: bfloat16 [28672, 64], P('tensor'), may hold values from -0.03125 to 0.03125
- proj_out: bfloat16 [8192, 64], P('tensor'), may hold values from -0.0625 to 0.0625
- lengths: int32 [256], P('dp'), may hold values from 1 to 128
- queries: bfloat16 [2048, 4096], P(('tensor', 'dp')), may hold values from -0.0078125 to 0.0078125
Outputs:
- scores: float32 [256, 2048], P('dp', 'tensor')
The draws below stay inside these ranges and needn't reach their ends.
All inputs are finite; a program needn't handle non-finite values.
Results may differ from the reference program's by a relative error of at most 0.005.
Values may be sent and summed in bfloat16 or wider, within the bound.
A program may use at most 64 MiB of HBM per device.

```python
import jax
import jax.numpy as jnp
from jax import lax

INNER = 28672
MODEL = 8192
RANK_IN = 64
RANK_OUT = 64
QUERIES = 2048
SEQ_LEN = 128
SEQS = 256


def with_ends(entries, rng, least, high):
    extent = entries.shape
    spot = [jax.random.randint(jax.random.fold_in(rng, axis), (), 0, extent[axis]) for axis in range(len(extent))]
    entries = entries.at[tuple(spot)].set(least)
    longest = extent.index(max(extent))
    spot[longest] = (spot[longest] + 1) % extent[longest]
    return entries.at[tuple(spot)].set(high)


def block_levels(key, extent, shards, least, top_value):
    level = 1.0
    for dim, parts in shards:
        draws = jax.random.uniform(jax.random.fold_in(jax.random.fold_in(key, 6), dim), (parts,), jnp.float32, least / len(shards), top_value / len(shards))
        level = level * jnp.repeat(jnp.exp(draws), extent[dim] // parts).reshape((-1,) + (1,) * (len(extent) - 1 - dim))
    return level


def gaussian(rng, dims, scale, limit, shards=(), kind=jnp.bfloat16):
    values = jax.random.normal(rng, dims, jnp.float32) * scale
    if len(shards) > 0:
        values = block_levels(rng, dims, shards, -0.22, 0.18) * values
    return jnp.clip(values, min=-limit, max=limit).astype(kind)


def setup_inputs(seed: int = 0) -> dict:
    key_list = jax.random.split(jax.random.key(seed), 7)
    return {
        "inputs": gaussian(key_list[0], (SEQS, SEQ_LEN, INNER), 1.0, 6.0, ((0, 8), (2, 32))),
        "out_grads": gaussian(key_list[1], (SEQS, SEQ_LEN, MODEL), 1.0, 6.0, ((0, 8), (2, 32))),
        "proj_in": gaussian(key_list[2], (INNER, RANK_IN), INNER ** -0.5, 0.03125, ((0, 32),)),
        "proj_out": gaussian(key_list[3], (MODEL, RANK_OUT), MODEL ** -0.5, 0.0625, ((0, 32),)),
        "lengths": with_ends(jax.random.randint(key_list[4], (SEQS,), 1, SEQ_LEN + 1), jax.random.fold_in(key_list[4], 1), 1, SEQ_LEN).astype(jnp.int32),
        "queries": gaussian(key_list[5], (QUERIES, RANK_IN * RANK_OUT), (RANK_IN * RANK_OUT * SEQ_LEN) ** -0.5, 0.0078125, ((0, 256),)),
    }


def reference(inputs, out_grads, proj_in, proj_out, lengths, queries):
    seq_count = inputs.shape[0]
    flat_in = inputs.reshape(seq_count * SEQ_LEN, INNER)
    flat_out = out_grads.reshape(seq_count * SEQ_LEN, MODEL)
    proj_a = jnp.dot(flat_in, proj_in, preferred_element_type=jnp.float32).reshape(seq_count, SEQ_LEN, RANK_IN)
    proj_b = jnp.dot(flat_out, proj_out, preferred_element_type=jnp.float32).reshape(seq_count, SEQ_LEN, RANK_OUT)
    positions = jnp.arange(SEQ_LEN, dtype=jnp.int32)
    live_mask = (positions[None, :] < lengths[:, None]).astype(jnp.float32)
    small_a = (proj_a * live_mask[:, :, None]).astype(jnp.bfloat16)
    small_b = proj_b.astype(jnp.bfloat16)
    example = jnp.einsum("sli,slj->sij", small_a.astype(jnp.float32), small_b.astype(jnp.float32))
    example = example.reshape(seq_count, RANK_IN * RANK_OUT).astype(jnp.bfloat16)
    return lax.dot_general(example, queries, (((1,), (1,)), ((), ())), preferred_element_type=jnp.float32)
```

```python
import functools

import jax
import jax.numpy as jnp
from jax import lax
from jax.experimental import pallas as pl
from jax.experimental.pallas import tpu as pltpu
from jax.sharding import PartitionSpec as P

MESH = pl.DeviceIdType.MESH
F32 = jnp.float32
BF16 = jnp.bfloat16
NX = 4


def encode(value):
    return (value * jnp.abs(value)).astype(BF16)


def decode(code):
    wide = code.astype(F32)
    root = jnp.sqrt(jnp.abs(wide))
    return jnp.where(wide < 0, -root, root)


def split(value):
    high = value.astype(BF16)
    return high, (value - high.astype(F32)).astype(BF16)


def kernel(
    nz, nd,
    x_hbm, g_hbm, wi_hbm, wo_hbm, len_ref, q_hbm, out_ref,
    xbuf, gbuf, wi, wo, w, raw, comb, keep, chain_in, final_in, z_out, z_in, qall, qflat, exall, exwide, small,
    load_sem, w_sem, raw_send, comb_send, chain_recv, final_recv, z_send, z_recv,
    q_send, q_recv, q_local, ex_send, ex_recv, fw_send,
):
    half = nz // 2
    tokens, rank = x_hbm.shape[1], wi_hbm.shape[1]
    feats = x_hbm.shape[2]
    t = lax.axis_index("tensor")
    d = lax.axis_index("dp")
    x, z = t // nz, t % nz
    x_right, x_left, x_far = (x + 1) % NX, (x + NX - 1) % NX, (x + 2) % NX
    right, left, far = x_right * nz + z, x_left * nz + z, x_far * nz + z

    def at_x(index):
        return {"tensor": index, "dp": d}

    def peer_z(k):
        return x * nz + (z + k) % nz

    barrier = pltpu.get_barrier_semaphore()
    partners = [at_x(right), at_x(left), at_x(far)]
    partners += [at_x(peer_z(k)) for k in range(1, nz)]
    partners += [{"tensor": t, "dp": (d + k) % nd} for k in range(1, nd)]
    for partner in partners:
        pl.semaphore_signal(barrier, inc=1, device_id=partner, device_id_type=MESH)

    w_copies = [
        pltpu.make_async_copy(wi_hbm, wi, w_sem.at[0]),
        pltpu.make_async_copy(wo_hbm, wo, w_sem.at[1]),
    ]
    for copy in w_copies:
        copy.start()

    loads = []
    for i in range(half):
        even, odd = (z + half + i) % nz, (z + half - 1 - i) % nz
        order = [
            (x_far, even), (x_far, odd), (x_right, odd), (x_left, even),
            (x_right, even), (x_left, odd), (x, even), (x, odd),
        ]
        for k, (xd, zd) in enumerate(order):
            slot = i * 8 + k
            s = xd * nz + zd
            loads.append((
                pltpu.make_async_copy(x_hbm.at[s], xbuf.at[slot], load_sem.at[0, slot]),
                pltpu.make_async_copy(g_hbm.at[s], gbuf.at[slot], load_sem.at[1, slot]),
            ))
            for copy in loads[-1]:
                copy.start()
    own_q = pltpu.make_async_copy(q_hbm, qall.at[d], q_local)
    own_q.start()

    for copy in w_copies:
        copy.wait()
    w[0:feats, :] = jnp.concatenate([wi[...], jnp.zeros_like(wi)], axis=1)
    w[feats:, :] = jnp.concatenate([jnp.zeros_like(wo), wo[...]], axis=1)

    def project(i, group):
        first = i * 8 + group * 4
        for slot in range(first, first + 4):
            for copy in loads[slot]:
                copy.wait()
        xs = xbuf[first:first + 4].reshape(4 * tokens, feats)
        gs = gbuf[first:first + 4].reshape(4 * tokens, gbuf.shape[2])
        total = jnp.dot(xs, w[0:feats, :], preferred_element_type=F32)
        total += jnp.dot(gs, w[feats:, :], preferred_element_type=F32)
        return total.reshape(4, tokens, 2 * rank)

    def remote(src, dst, send, recv, device):
        return pltpu.make_async_remote_copy(
            src_ref=src, dst_ref=dst, send_sem=send, recv_sem=recv, device_id=device, device_id_type=MESH
        )

    raw_copies, comb_copies = {}, {}

    def first_sends(i):
        raw[i] = encode(project(i, 0))
        raw_copies[i] = [
            remote(raw.at[i, 0], chain_in.at[0, i], raw_send.at[i, 0], chain_recv.at[0, i], at_x(right)),
            remote(raw.at[i, 1], chain_in.at[1, i], raw_send.at[i, 1], chain_recv.at[1, i], at_x(left)),
            remote(raw.at[i, 2], final_in.at[0, i, 1], raw_send.at[i, 2], final_recv.at[0, i, 1], at_x(right)),
            remote(raw.at[i, 3], final_in.at[1, i, 0], raw_send.at[i, 3], final_recv.at[1, i, 0], at_x(left)),
        ]
        for copy in raw_copies[i]:
            copy.start()

    def combine(i):
        comb_copies[i] = []
        for side in range(2):
            raw_copies[i][side].wait_recv()
            comb[i, side] = encode(keep[i, side] + decode(chain_in[side, i]))
            copy = remote(
                comb.at[i, side], final_in.at[side, i, side], comb_send.at[i, side], final_recv.at[side, i, side],
                at_x(right if side == 0 else left),
            )
            copy.start()
            comb_copies[i].append(copy)

    z_copies = {}

    def reduce_x(i):
        for parity in range(2):
            k = half + i if parity == 0 else half - 1 - i
            comb_copies[i][parity].wait_recv()
            raw_copies[i][3 - parity].wait_recv()
            total = keep[i, 2 + parity] + decode(final_in[0, i, parity]) + decode(final_in[1, i, parity])
            if k == 0:
                keep[i, 2 + parity] = total
                continue
            z_out[k - 1] = encode(total)
            z_copies[k] = remote(
                z_out.at[k - 1], z_in.at[k - 1], z_send.at[k - 1], z_recv.at[k - 1], at_x(peer_z(k))
            )
            z_copies[k].start()

    q_copies = []
    for i in range(half + 2):
        if i == 0:
            raw_first = None
            pl.semaphore_wait(barrier, len(partners))
        if i < half:
            first_sends(i)
        if i == 0:
            for k in range(1, nd):
                copy = remote(
                    q_hbm, qall.at[d], q_send.at[k - 1], q_recv.at[k - 1], {"tensor": t, "dp": (d + k) % nd}
                )
                copy.start()
                q_copies.append(copy)
        if 1 <= i <= half:
            combine(i - 1)
        if i < half:
            keep[i] = project(i, 1)
        if i >= 2:
            reduce_x(i - 2)

    own_q.wait()
    for copy in q_copies:
        copy.wait()
    for k in range(nd):
        small_rows = qall.shape[1]
        if k % 2 == 0:
            qflat[k * small_rows:(k + 2) * small_rows, :] = jnp.concatenate([qall[k], qall[k + 1]], axis=0)

    total = keep[half - 1, 3]
    for i in range(half):
        for k in (half + i, half - 1 - i):
            if k > 0:
                z_copies[k].wait_recv()
                total += decode(z_in[k - 1])

    live = (lax.broadcasted_iota(jnp.int32, (tokens, 2 * rank), 0) < len_ref[t]).astype(F32)
    lane = lax.broadcasted_iota(jnp.int32, (tokens, 2 * rank), 1)
    both = jnp.where(lane < rank, pltpu.roll(total, rank, 1), total)
    a_high, a_low = split(total * live)
    b_high, b_low = split(both)

    def outer(left_side, right_side):
        return lax.dot_general(left_side, right_side, (((0,), (0,)), ((), ())), preferred_element_type=F32)

    small[...] = (outer(a_high, b_high) + (outer(a_high, b_low) + outer(a_low, b_high)))[0:rank]
    rows = rank // 2
    lane_half = lax.broadcasted_iota(jnp.int32, (rows, 2 * rank), 1)
    example = jnp.where(lane_half < rank, small[pl.ds(0, rows, stride=2), :], small[pl.ds(1, rows, stride=2), :])
    exall[t] = example.astype(BF16)

    ex_copies = []
    for k in range(1, nz):
        copy = remote(exall.at[t], exall.at[t], ex_send.at[k - 1], ex_recv.at[0, k], at_x(peer_z(k)))
        copy.start()
        ex_copies.append(copy)
    fw_copies = []
    for j, k in enumerate([0] + [k for m in range(1, half + 1) for k in ((m, nz - m) if m < half else (m,))]):
        source = x * nz + (z + nz - k) % nz
        if k > 0:
            ex_copies[k - 1].wait_recv()
        for side, device in enumerate((right, left, far)):
            copy = remote(
                exall.at[source], exall.at[source], fw_send.at[side, k], ex_recv.at[1 + side, k], at_x(device)
            )
            copy.start()
            fw_copies.append(copy)
    for copy in fw_copies:
        copy.wait_recv()

    count = exall.shape[0]
    exwide[...] = exall[...].reshape(count * rows, 2 * rank).astype(F32)
    flat = jnp.concatenate([exwide[pl.ds(r, count, stride=rows), :] for r in range(rows)], axis=1)
    out_ref[...] = lax.dot_general(
        flat.astype(BF16), qflat[...], (((1,), (1,)), ((), ())), preferred_element_type=F32
    )

    for copies in list(raw_copies.values()) + list(comb_copies.values()):
        for copy in copies:
            copy.wait_send()
    for copy in list(z_copies.values()) + ex_copies + fw_copies:
        copy.wait_send()


def solution(mesh):
    nt, nd = mesh.shape["tensor"], mesh.shape["dp"]
    nz = nt // NX
    half = nz // 2

    def body(inputs, out_grads, proj_in, proj_out, lengths, queries):
        seqs, tokens, feats = inputs.shape
        grads = out_grads.shape[2]
        rank = proj_in.shape[1]
        lanes = 2 * rank
        block = (tokens, lanes)
        dma = pltpu.SemaphoreType.DMA
        return pl.pallas_call(
            functools.partial(kernel, nz, nd),
            out_shape=jax.ShapeDtypeStruct((seqs, nd * queries.shape[0]), F32),
            in_specs=[
                pl.BlockSpec(memory_space=pl.ANY),
                pl.BlockSpec(memory_space=pl.ANY),
                pl.BlockSpec(memory_space=pl.ANY),
                pl.BlockSpec(memory_space=pl.ANY),
                pl.BlockSpec(memory_space=pltpu.SMEM),
                pl.BlockSpec(memory_space=pl.ANY),
            ],
            out_specs=pl.BlockSpec(memory_space=pltpu.VMEM),
            scratch_shapes=[
                pltpu.VMEM((seqs, tokens, feats), BF16),
                pltpu.VMEM((seqs, tokens, grads), BF16),
                pltpu.VMEM((feats, rank), BF16),
                pltpu.VMEM((grads, rank), BF16),
                pltpu.VMEM((feats + grads, lanes), BF16),
                pltpu.VMEM((half, 4) + block, BF16),
                pltpu.VMEM((half, 2) + block, BF16),
                pltpu.VMEM((half, 4) + block, F32),
                pltpu.VMEM((2, half) + block, BF16),
                pltpu.VMEM((2, half, 2) + block, BF16),
                pltpu.VMEM((nz - 1,) + block, BF16),
                pltpu.VMEM((nz - 1,) + block, BF16),
                pltpu.VMEM((nd,) + queries.shape, BF16),
                pltpu.VMEM((nd * queries.shape[0], queries.shape[1]), BF16),
                pltpu.VMEM((seqs, rank // 2, lanes), BF16),
                pltpu.VMEM((seqs * rank // 2, lanes), F32),
                pltpu.VMEM((rank, lanes), F32),
                dma((2, seqs)),
                dma((2,)),
                dma((half, 4)),
                dma((half, 2)),
                dma((2, half)),
                dma((2, half, 2)),
                dma((nz - 1,)),
                dma((nz - 1,)),
                dma((nd - 1,)),
                dma((nd - 1,)),
                dma,
                dma((nz - 1,)),
                dma((4, nz)),
                dma((3, nz)),
            ],
            compiler_params=pltpu.CompilerParams(
                collective_id=0, has_side_effects=True, vmem_limit_bytes=48 * 1024 * 1024
            ),
        )(inputs, out_grads, proj_in, proj_out, lengths, queries)

    return jax.shard_map(
        body,
        mesh=mesh,
        in_specs=(
            P("dp", None, "tensor"),
            P("dp", None, "tensor"),
            P("tensor", None),
            P("tensor", None),
            P("dp"),
            P(("tensor", "dp"), None),
        ),
        out_specs=P("dp", "tensor"),
        check_vma=False,
    )
```

```python
import functools

import jax
import jax.numpy as jnp
from jax import lax
from jax.experimental import pallas as pl
from jax.experimental.pallas import tpu as pltpu
from jax.sharding import PartitionSpec as P

MESH = pl.DeviceIdType.MESH
F32 = jnp.float32
BF16 = jnp.bfloat16
NX = 4


def encode(value):
    return (value * jnp.abs(value)).astype(BF16)


def decode(code):
    wide = code.astype(F32)
    root = jnp.sqrt(jnp.abs(wide))
    return jnp.where(wide < 0, -root, root)


def split(value):
    high = value.astype(BF16)
    return high, (value - high.astype(F32)).astype(BF16)


def hops(steps, size):
    return min(steps, size - steps)


def kernel(
    nz, nd,
    x_hbm, g_hbm, wi_hbm, wo_hbm, len_hbm, q_hbm, out_ref,
    acts, wt, w, len_ref, sent, keep, chain_in, final_in, z_out, z_in, qall, qflat, exall, exwide, small,
    load_sem, w_sem, len_sem, own_q_sem, x_send, z_send, q_send, ex_send, chain_recv, final_recv, z_recv, q_recv, ex_recv,
):
    half = nz // 2
    tokens, rank = x_hbm.shape[1], wi_hbm.shape[0]
    feats = x_hbm.shape[2]
    t = lax.axis_index("tensor")
    d = lax.axis_index("dp")
    x, z = t // nz, t % nz
    x_right, x_left, x_far = (x + 1) % NX, (x + NX - 1) % NX, (x + 2) % NX

    def peer(dx, dz):
        return {"tensor": ((x + dx) % NX) * nz + (z + dz) % nz, "dp": d}

    right, left = peer(1, 0), peer(NX - 1, 0)
    barrier = pltpu.get_barrier_semaphore()
    partners = [right, left]
    partners += [peer(0, k) for k in range(1, nz)]
    partners += [{"tensor": t, "dp": (d + k) % nd} for k in range(1, nd)]
    for partner in partners:
        pl.semaphore_signal(barrier, inc=1, device_id=partner, device_id_type=MESH)

    offsets = [(half + i, half - 1 - i) for i in range(half)]
    first_group, second_group = [], []
    for even, odd in offsets:
        ze, zo = (z + even) % nz, (z + odd) % nz
        first_group.append([(x_far, ze), (x_far, zo), (x_right, zo), (x_left, ze)])
        second_group.append([(x_right, ze), (x_left, zo), (x, ze), (x, zo)])

    wt[...] = jnp.zeros_like(wt)
    pltpu.make_async_copy(wi_hbm, wt.at[0:rank, 0:feats], w_sem).start()
    pltpu.make_async_copy(wo_hbm, wt.at[rank:2 * rank, feats:], w_sem).start()
    for group, owners in enumerate(first_group + second_group):
        for k, (xd, zd) in enumerate(owners):
            s, slot = xd * nz + zd, group * 4 + k
            pltpu.make_async_copy(x_hbm.at[s], acts.at[slot, :, 0:feats], load_sem.at[group]).start()
            pltpu.make_async_copy(g_hbm.at[s], acts.at[slot, :, feats:], load_sem.at[group]).start()
    own_q = pltpu.make_async_copy(q_hbm, qall.at[d], own_q_sem)
    own_q.start()
    own_len = pltpu.make_async_copy(len_hbm, len_ref, len_sem)
    own_len.start()

    def drain(ref, sem):
        pltpu.make_async_copy(ref, ref, sem).wait()

    drain(wt.at[0:rank], w_sem)
    w[...] = wt[...].T

    def project(group):
        block = acts.at[group * 4:group * 4 + 4]
        drain(block, load_sem.at[group])
        rows = block[...].reshape(4 * tokens, block.shape[2])
        return jnp.dot(rows, w[...], preferred_element_type=F32).reshape(4, tokens, 2 * rank)

    def send(src, dst, send_sem, recv_sem, device):
        pltpu.make_async_remote_copy(
            src_ref=src, dst_ref=dst, send_sem=send_sem, recv_sem=recv_sem, device_id=device, device_id_type=MESH
        ).start()

    def send_far(i):
        for side, device in enumerate((right, left)):
            send(sent.at[i, side], chain_in.at[i, side], x_send, chain_recv.at[i, side], device)

    def send_raw(i):
        send(sent.at[i, 2], final_in.at[i, 1, 0], x_send, final_recv.at[i], right)
        send(sent.at[i, 3], final_in.at[i, 0, 1], x_send, final_recv.at[i], left)

    def combine(i):
        for side, device in enumerate((right, left)):
            drain(chain_in.at[i, side], chain_recv.at[i, side])
            sent[i, 4 + side] = encode(keep[i, side] + decode(chain_in[i, side]))
            send(sent.at[i, 4 + side], final_in.at[i, side, side], x_send, final_recv.at[i], device)

    def reduce_x(i):
        drain(final_in.at[i], final_recv.at[i])
        for parity, k in enumerate(offsets[i]):
            total = keep[i, 2 + parity] + (decode(final_in[i, parity, 0]) + decode(final_in[i, parity, 1]))
            if k == 0:
                return total
            z_out[k - 1] = encode(total)
            send(z_out.at[k - 1], z_in.at[k - 1], z_send, z_recv, peer(0, k))

    for i in range(half):
        sent[i, 0:4] = encode(project(i))
    pl.semaphore_wait(barrier, len(partners))
    send_far(0)
    if half > 1:
        send_far(1)
    send_raw(0)
    for i in range(2, half):
        send_far(i)
        send_raw(i - 1)
    for i in range(half):
        keep[i] = project(half + i)
        combine(i)
        if i == 0 and half > 1:
            send_raw(half - 1)
        if i == 0:
            for k in range(1, nd):
                send(q_hbm, qall.at[d], q_send, q_recv, {"tensor": t, "dp": (d + k) % nd})
    for i in range(half):
        total = reduce_x(i)

    own_q.wait()
    own_len.wait()
    drain(qall.at[0:nd - 1], q_recv)
    rows = qall.shape[1]
    for k in range(0, nd, 2):
        qflat[k * rows:(k + 2) * rows, :] = jnp.concatenate([qall[k], qall[k + 1]], axis=0)

    drain(z_in, z_recv)
    for k in range(nz - 1):
        total += decode(z_in[k])

    live = (lax.broadcasted_iota(jnp.int32, (tokens, 2 * rank), 0) < len_ref[t]).astype(F32)
    lane = lax.broadcasted_iota(jnp.int32, (tokens, 2 * rank), 1)
    both = jnp.where(lane < rank, pltpu.roll(total, rank, 1), total)
    a_high, a_low = split(total * live)
    b_high, b_low = split(both)

    def outer(left_side, right_side):
        return lax.dot_general(left_side, right_side, (((0,), (0,)), ((), ())), preferred_element_type=F32)

    small[...] = (outer(a_high, b_high) + (outer(a_high, b_low) + outer(a_low, b_high)))[0:rank]
    pairs = rank // 2
    lane_half = lax.broadcasted_iota(jnp.int32, (pairs, 2 * rank), 1)
    example = jnp.where(lane_half < rank, small[pl.ds(0, pairs, stride=2), :], small[pl.ds(1, pairs, stride=2), :])
    exall[t] = example.astype(BF16)

    others = [(dx, dz) for dx in range(NX) for dz in range(nz) if (dx, dz) != (0, 0)]
    others.sort(key=lambda step: -(hops(step[0], NX) + hops(step[1], nz)))
    for dx, dz in others:
        send(exall.at[t], exall.at[t], ex_send, ex_recv, peer(dx, dz))
    count = exall.shape[0]
    drain(exall.at[0:count - 1], ex_recv)

    exwide[...] = exall[...].reshape(count * pairs, 2 * rank).astype(F32)
    flat = jnp.concatenate([exwide[pl.ds(r, count, stride=pairs), :] for r in range(pairs)], axis=1)
    out_ref[...] = lax.dot_general(
        flat.astype(BF16), qflat[...], (((1,), (1,)), ((), ())), preferred_element_type=F32
    )

    drain(sent, x_send)
    drain(z_out, z_send)
    drain(qall.at[0:nd - 1], q_send)
    drain(exall.at[0:count - 1], ex_send)


def solution(mesh):
    nt, nd = mesh.shape["tensor"], mesh.shape["dp"]
    nz = nt // NX
    half = nz // 2

    def body(inputs, out_grads, proj_in, proj_out, lengths, queries):
        seqs, tokens, feats = inputs.shape
        grads = out_grads.shape[2]
        rank = proj_in.shape[1]
        lanes = 2 * rank
        block = (tokens, lanes)
        dma = pltpu.SemaphoreType.DMA
        return pl.pallas_call(
            functools.partial(kernel, nz, nd),
            out_shape=jax.ShapeDtypeStruct((seqs, nd * queries.shape[0]), F32),
            in_specs=[pl.BlockSpec(memory_space=pltpu.HBM)] * 6,
            out_specs=pl.BlockSpec(memory_space=pltpu.VMEM),
            scratch_shapes=[
                pltpu.VMEM((seqs, tokens, feats + grads), BF16),
                pltpu.VMEM((lanes, feats + grads), BF16),
                pltpu.VMEM((feats + grads, lanes), BF16),
                pltpu.SMEM(lengths.shape, jnp.int32),
                pltpu.VMEM((half, 6) + block, BF16),
                pltpu.VMEM((half, 4) + block, F32),
                pltpu.VMEM((half, 2) + block, BF16),
                pltpu.VMEM((half, 2, 2) + block, BF16),
                pltpu.VMEM((nz - 1,) + block, BF16),
                pltpu.VMEM((nz - 1,) + block, BF16),
                pltpu.VMEM((nd,) + queries.shape, BF16),
                pltpu.VMEM((nd * queries.shape[0], queries.shape[1]), BF16),
                pltpu.VMEM((seqs, rank // 2, lanes), BF16),
                pltpu.VMEM((seqs * rank // 2, lanes), F32),
                pltpu.VMEM((rank, lanes), F32),
                dma((nz,)),
            ] + [dma] * 7 + [dma((half, 2)), dma((half,))] + [dma] * 3,
            compiler_params=pltpu.CompilerParams(
                collective_id=0, has_side_effects=True, vmem_limit_bytes=60 * 1024 * 1024
            ),
        )(inputs, out_grads, proj_in.T, proj_out.T, lengths, queries)

    return jax.shard_map(
        body,
        mesh=mesh,
        in_specs=(
            P("dp", None, "tensor"),
            P("dp", None, "tensor"),
            P("tensor", None),
            P("tensor", None),
            P("dp"),
            P(("tensor", "dp"), None),
        ),
        out_specs=P("dp", "tensor"),
        check_vma=False,
    )
```

```python
import functools

import jax
import jax.numpy as jnp
from jax import lax
from jax.experimental import pallas as pl
from jax.experimental.pallas import tpu as pltpu
from jax.sharding import PartitionSpec as P

MESH = pl.DeviceIdType.MESH
F32 = jnp.float32
BF16 = jnp.bfloat16
NX = 4


def encode(value):
    return (value * jnp.abs(value)).astype(BF16)


def decode(code):
    wide = code.astype(F32)
    root = jnp.sqrt(jnp.abs(wide))
    return jnp.where(wide < 0, -root, root)


def split(value):
    high = value.astype(BF16)
    return high, (value - high.astype(F32)).astype(BF16)


def hops(steps, size):
    return min(steps, size - steps)


def kernel(
    nz, nd,
    x_hbm, g_hbm, wi_hbm, wo_hbm, len_hbm, q_hbm, out_ref,
    acts, wt, w, len_ref, sent, keep, chain_in, final_in, z_out, z_in, qall, qflat, exall, exwide, small,
    load_sem, w_sem, len_sem, own_q_sem, in_sem, x_send, z_send, q_send, ex_send, chain_recv, final_recv, z_recv, q_recv, ex_recv,
):
    half = nz // 2
    tokens, rank = x_hbm.shape[1], wi_hbm.shape[0]
    feats = x_hbm.shape[2]
    t = lax.axis_index("tensor")
    d = lax.axis_index("dp")
    x, z = t // nz, t % nz
    x_right, x_left, x_far = (x + 1) % NX, (x + NX - 1) % NX, (x + 2) % NX

    def peer(dx, dz):
        return {"tensor": ((x + dx) % NX) * nz + (z + dz) % nz, "dp": d}

    right, left = peer(1, 0), peer(NX - 1, 0)
    core, y, ny = d % 2, d // 2, nd // 2

    def peer_y(dy, side):
        return {"tensor": t, "dp": ((y + dy) % ny) * 2 + side}

    barrier = pltpu.get_barrier_semaphore()
    partners = [right, left]
    partners += [peer(0, k) for k in range(1, nz)]
    partners += [peer_y(k, core) for k in range(1, ny)]
    for partner in partners:
        pl.semaphore_signal(barrier, inc=1, device_id=partner, device_id_type=MESH)

    @pl.when(core == 0)
    def _():
        for k in range(ny):
            pl.semaphore_signal(barrier, inc=1, device_id=peer_y(k, 1), device_id_type=MESH)

    offsets = [(half + i, half - 1 - i) for i in range(half)]
    chunks = [[], [], [], [], [], []]
    early = (half + 1) // 2
    for i, (even, odd) in enumerate(offsets):
        ze, zo = (z + even) % nz, (z + odd) % nz
        chunks[0 if i < early else 2] += [(x_far, ze), (x_far, zo)]
        chunks[1 if i < early else 4] += [(x_right, zo), (x_left, ze)]
        chunks[3] += [(x_right, ze), (x_left, zo)]
        chunks[5] += [(x, ze), (x, zo)]

    wt[...] = jnp.zeros_like(wt)
    pltpu.make_async_copy(wi_hbm, wt.at[0:rank, 0:feats], w_sem).start()
    pltpu.make_async_copy(wo_hbm, wt.at[rank:2 * rank, feats:], w_sem).start()
    starts = [0]
    for c, owners in enumerate(chunks):
        for k, (xd, zd) in enumerate(owners):
            s, slot = xd * nz + zd, starts[c] + k
            pltpu.make_async_copy(x_hbm.at[s], acts.at[slot, :, 0:feats], load_sem.at[c]).start()
            pltpu.make_async_copy(g_hbm.at[s], acts.at[slot, :, feats:], load_sem.at[c]).start()
        starts.append(starts[c] + len(owners))
    own_q = pltpu.make_async_copy(q_hbm, qall.at[d], own_q_sem)
    own_q.start()
    own_len = pltpu.make_async_copy(len_hbm, len_ref, len_sem)
    own_len.start()

    def drain(ref, sem):
        pltpu.make_async_copy(ref, ref, sem).wait()

    drain(wt.at[0:rank], w_sem)
    w[...] = wt[...].T

    def project(c):
        count = starts[c + 1] - starts[c]
        block = acts.at[starts[c]:starts[c + 1]]
        drain(block, load_sem.at[c])
        total = jnp.dot(
            block[:, :, 0:feats].reshape(count * tokens, feats), w[0:feats, :], preferred_element_type=F32
        )
        total += jnp.dot(
            block[:, :, feats:].reshape(count * tokens, block.shape[2] - feats), w[feats:, :], preferred_element_type=F32
        )
        return total.reshape(count // 2, 2, tokens, 2 * rank)

    def send(src, dst, send_sem, recv_sem, device):
        pltpu.make_async_remote_copy(
            src_ref=src, dst_ref=dst, send_sem=send_sem, recv_sem=recv_sem, device_id=device, device_id_type=MESH
        ).start()

    def send_far(i):
        for side, device in enumerate((right, left)):
            send(sent.at[0, i, side], chain_in.at[i, side], x_send, chain_recv.at[i, side], device)

    def send_raw(i):
        send(sent.at[1, i, 0], final_in.at[i, 1, 0], x_send, final_recv.at[i], right)
        send(sent.at[1, i, 1], final_in.at[i, 0, 1], x_send, final_recv.at[i], left)

    def combine(i):
        for side, device in enumerate((right, left)):
            drain(chain_in.at[i, side], chain_recv.at[i, side])
            sent[2, i, side] = encode(keep[0, i, side] + decode(chain_in[i, side]))
            send(sent.at[2, i, side], final_in.at[i, side, side], x_send, final_recv.at[i], device)

    def reduce_x(i):
        drain(final_in.at[i], final_recv.at[i])
        for parity, k in enumerate(offsets[i]):
            total = keep[1, i, parity] + (decode(final_in[i, parity, 0]) + decode(final_in[i, parity, 1]))
            if k == 0:
                return total
            z_out[k - 1] = encode(total)
            send(z_out.at[k - 1], z_in.at[k - 1], z_send, z_recv.at[k - 1], peer(0, k))

    def send_queries():
        for k in range(1, ny):
            send(q_hbm, qall.at[d], q_send, q_recv, peer_y(k, core))

        @pl.when(core == 1)
        def _():
            for k in range(ny):
                pl.semaphore_signal(in_sem, inc=1, device_id=peer_y(k, 0), device_id_type=MESH)
                send(q_hbm, qall.at[d], q_send, q_recv, peer_y(k, 0))

    sent[0, 0:early] = encode(project(0))
    pl.semaphore_wait(barrier, len(partners) + core * ny)
    for i in range(early):
        send_far(i)
    sent[1, 0:early] = encode(project(1))
    send_raw(0)
    sent[0, early:] = encode(project(2))
    send_far(early)
    keep[0] = project(3)
    combine(0)
    for i in range(1, early):
        send_raw(i)
        combine(i)
    for i in range(early + 1, half):
        send_far(i)
    sent[1, early:] = encode(project(4))
    send_raw(early)
    combine(early)
    for i in range(early + 1, half):
        send_raw(i)
    send_queries()
    keep[1] = project(5)
    for i in range(early):
        reduce_x(i)
    for i in range(early + 1, half):
        combine(i)
    for i in range(early, half):
        total = reduce_x(i)

    @pl.when(core == 0)
    def _():
        pl.semaphore_wait(in_sem, ny)
        for k in range(ny):
            send(q_hbm, qall.at[d], q_send, q_recv, peer_y(k, 1))

    for k in (k for pair in offsets for k in pair if k > 0):
        drain(z_in.at[k - 1], z_recv.at[k - 1])
        total += decode(z_in[k - 1])

    own_len.wait()
    live = (lax.broadcasted_iota(jnp.int32, (tokens, 2 * rank), 0) < len_ref[t]).astype(F32)
    lane = lax.broadcasted_iota(jnp.int32, (tokens, 2 * rank), 1)
    both = jnp.where(lane < rank, pltpu.roll(total, rank, 1), total)
    a_high, a_low = split(total * live)
    b_high, b_low = split(both)

    def outer(left_side, right_side):
        return lax.dot_general(left_side, right_side, (((0,), (0,)), ((), ())), preferred_element_type=F32)

    small[...] = (outer(a_high, b_high) + (outer(a_high, b_low) + outer(a_low, b_high)))[0:rank]
    pairs = rank // 2
    lane_half = lax.broadcasted_iota(jnp.int32, (pairs, 2 * rank), 1)
    example = jnp.where(lane_half < rank, small[pl.ds(0, pairs, stride=2), :], small[pl.ds(1, pairs, stride=2), :])
    exall[t] = example.astype(BF16)

    others = [(dx, dz) for dx in range(NX) for dz in range(nz) if (dx, dz) != (0, 0)]
    others.sort(key=lambda step: -(hops(step[0], NX) + hops(step[1], nz)))
    for dx, dz in others:
        send(exall.at[t], exall.at[t], ex_send, ex_recv, peer(dx, dz))
    count = exall.shape[0]

    own_q.wait()
    drain(qall.at[0:nd - 1], q_recv)
    rows = qall.shape[1]
    for k in range(0, nd, 2):
        qflat[k * rows:(k + 2) * rows, :] = jnp.concatenate([qall[k], qall[k + 1]], axis=0)

    drain(exall.at[0:count - 1], ex_recv)

    exwide[...] = exall[...].reshape(count * pairs, 2 * rank).astype(F32)
    flat = jnp.concatenate([exwide[pl.ds(r, count, stride=pairs), :] for r in range(pairs)], axis=1)
    out_ref[...] = lax.dot_general(
        flat.astype(BF16), qflat[...], (((1,), (1,)), ((), ())), preferred_element_type=F32
    )

    drain(sent, x_send)
    drain(z_out, z_send)
    drain(qall.at[0:nd - 1], q_send)
    drain(exall.at[0:count - 1], ex_send)


def solution(mesh):
    nt, nd = mesh.shape["tensor"], mesh.shape["dp"]
    nz = nt // NX
    half = nz // 2

    def body(inputs, out_grads, proj_in, proj_out, lengths, queries):
        seqs, tokens, feats = inputs.shape
        grads = out_grads.shape[2]
        rank = proj_in.shape[1]
        lanes = 2 * rank
        block = (tokens, lanes)
        dma = pltpu.SemaphoreType.DMA
        return pl.pallas_call(
            functools.partial(kernel, nz, nd),
            out_shape=jax.ShapeDtypeStruct((seqs, nd * queries.shape[0]), F32),
            in_specs=[pl.BlockSpec(memory_space=pltpu.HBM)] * 6,
            out_specs=pl.BlockSpec(memory_space=pltpu.VMEM),
            scratch_shapes=[
                pltpu.VMEM((seqs, tokens, feats + grads), BF16),
                pltpu.VMEM((lanes, feats + grads), BF16),
                pltpu.VMEM((feats + grads, lanes), BF16),
                pltpu.SMEM(lengths.shape, jnp.int32),
                pltpu.VMEM((3, half, 2) + block, BF16),
                pltpu.VMEM((2, half, 2) + block, F32),
                pltpu.VMEM((half, 2) + block, BF16),
                pltpu.VMEM((half, 2, 2) + block, BF16),
                pltpu.VMEM((nz - 1,) + block, BF16),
                pltpu.VMEM((nz - 1,) + block, BF16),
                pltpu.VMEM((nd,) + queries.shape, BF16),
                pltpu.VMEM((nd * queries.shape[0], queries.shape[1]), BF16),
                pltpu.VMEM((seqs, rank // 2, lanes), BF16),
                pltpu.VMEM((seqs * rank // 2, lanes), F32),
                pltpu.VMEM((rank, lanes), F32),
                dma((6,)),
            ] + [dma] * 3 + [pltpu.SemaphoreType.REGULAR] + [dma] * 4 + [dma((half, 2)), dma((half,)), dma((nz - 1,))] + [dma] * 2,
            compiler_params=pltpu.CompilerParams(
                collective_id=0, has_side_effects=True, vmem_limit_bytes=60 * 1024 * 1024
            ),
        )(inputs, out_grads, proj_in.T, proj_out.T, lengths, queries)

    return jax.shard_map(
        body,
        mesh=mesh,
        in_specs=(
            P("dp", None, "tensor"),
            P("dp", None, "tensor"),
            P("tensor", None),
            P("tensor", None),
            P("dp"),
            P(("tensor", "dp"), None),
        ),
        out_specs=P("dp", "tensor"),
        check_vma=False,
    )
```

```python
import functools

import jax
import jax.numpy as jnp
from jax import lax
from jax.experimental import pallas as pl
from jax.experimental.pallas import tpu as pltpu
from jax.sharding import PartitionSpec as P

MESH = pl.DeviceIdType.MESH
F32 = jnp.float32
BF16 = jnp.bfloat16
NX = 4


def encode(value):
    return (value * jnp.abs(value)).astype(BF16)


def decode(code):
    wide = code.astype(F32)
    root = jnp.sqrt(jnp.abs(wide))
    return jnp.where(wide < 0, -root, root)


def split(value):
    high = value.astype(BF16)
    return high, (value - high.astype(F32)).astype(BF16)


def hops(steps, size):
    return min(steps, size - steps)


def kernel(
    nz, nd,
    x_hbm, g_hbm, wi_hbm, wo_hbm, len_hbm, q_hbm, out_ref,
    acts, wt, w, len_ref, sent, keep, chain_in, final_in, z_out, z_in, qall, qflat, exall, exwide, small,
    load_sem, w_sem, len_sem, own_q_sem, in_core, in_z, x_send, z_send, q_send, ex_send, chain_recv, final_recv, z_recv, q_recv, ex_recv,
):
    half = nz // 2
    tokens, rank = x_hbm.shape[1], wi_hbm.shape[0]
    feats = x_hbm.shape[2]
    t = lax.axis_index("tensor")
    d = lax.axis_index("dp")
    x, z = t // nz, t % nz
    x_right, x_left, x_far = (x + 1) % NX, (x + NX - 1) % NX, (x + 2) % NX

    def peer(dx, dz):
        return {"tensor": ((x + dx) % NX) * nz + (z + dz) % nz, "dp": d}

    right, left = peer(1, 0), peer(NX - 1, 0)
    core, y, ny = d % 2, d // 2, nd // 2

    def peer_y(dy, side):
        return {"tensor": t, "dp": ((y + dy) % ny) * 2 + side}

    barrier = pltpu.get_barrier_semaphore()
    partners = [right, left]
    partners += [peer_y(k, core) for k in range(1, ny)]
    for partner in partners:
        pl.semaphore_signal(barrier, inc=1, device_id=partner, device_id_type=MESH)

    @pl.when(core == 0)
    def _():
        for k in range(ny):
            pl.semaphore_signal(barrier, inc=1, device_id=peer_y(k, 1), device_id_type=MESH)

    for k in range(1, nz):
        @pl.when(z + k < nz)
        def _(k=k):
            pl.semaphore_signal(barrier, inc=1, device_id=peer(0, k), device_id_type=MESH)

    offsets = [(half + i, half - 1 - i) for i in range(half)]
    chunks = [[], [], [], [], [], []]
    early = (half + 1) // 2
    for i, (even, odd) in enumerate(offsets):
        ze, zo = (z + even) % nz, (z + odd) % nz
        chunks[0 if i < early else 1] += [(x_far, ze), (x_far, zo)]
        chunks[2 if i < early else 4] += [(x_right, zo), (x_left, ze)]
        chunks[3] += [(x_right, ze), (x_left, zo)]
        chunks[5] += [(x, ze), (x, zo)]

    wt[...] = jnp.zeros_like(wt)
    pltpu.make_async_copy(wi_hbm, wt.at[0:rank, 0:feats], w_sem).start()
    pltpu.make_async_copy(wo_hbm, wt.at[rank:2 * rank, feats:], w_sem).start()
    starts = [0]
    for c, owners in enumerate(chunks):
        for k, (xd, zd) in enumerate(owners):
            s, slot = xd * nz + zd, starts[c] + k
            pltpu.make_async_copy(x_hbm.at[s], acts.at[slot, :, 0:feats], load_sem.at[c]).start()
            pltpu.make_async_copy(g_hbm.at[s], acts.at[slot, :, feats:], load_sem.at[c]).start()
        starts.append(starts[c] + len(owners))
    own_q = pltpu.make_async_copy(q_hbm, qall.at[d], own_q_sem)
    own_q.start()
    own_len = pltpu.make_async_copy(len_hbm, len_ref, len_sem)
    own_len.start()

    def drain(ref, sem):
        pltpu.make_async_copy(ref, ref, sem).wait()

    drain(wt.at[0:rank], w_sem)
    w[...] = wt[...].T

    def project(c):
        count = starts[c + 1] - starts[c]
        block = acts.at[starts[c]:starts[c + 1]]
        drain(block, load_sem.at[c])
        total = jnp.dot(
            block[:, :, 0:feats].reshape(count * tokens, feats), w[0:feats, :], preferred_element_type=F32
        )
        total += jnp.dot(
            block[:, :, feats:].reshape(count * tokens, block.shape[2] - feats), w[feats:, :], preferred_element_type=F32
        )
        return total.reshape(count // 2, 2, tokens, 2 * rank)

    def send(src, dst, send_sem, recv_sem, device):
        pltpu.make_async_remote_copy(
            src_ref=src, dst_ref=dst, send_sem=send_sem, recv_sem=recv_sem, device_id=device, device_id_type=MESH
        ).start()

    def send_far(i):
        for side, device in enumerate((right, left)):
            send(sent.at[0, i, side], chain_in.at[i, side], x_send, chain_recv.at[i, side], device)

    def send_raw(i):
        send(sent.at[1, i, 0], final_in.at[i, 1, 0], x_send, final_recv.at[i], right)
        send(sent.at[1, i, 1], final_in.at[i, 0, 1], x_send, final_recv.at[i], left)

    def combine(i):
        for side, device in enumerate((right, left)):
            drain(chain_in.at[i, side], chain_recv.at[i, side])
            sent[2, i, side] = encode(keep[0, i, side] + decode(chain_in[i, side]))
            send(sent.at[2, i, side], final_in.at[i, side, side], x_send, final_recv.at[i], device)

    def reduce_x(i):
        drain(final_in.at[i], final_recv.at[i])
        for parity, k in enumerate(offsets[i]):
            total = keep[1, i, parity] + (decode(final_in[i, parity, 0]) + decode(final_in[i, parity, 1]))
            if k == 0:
                return total
            z_out[k - 1] = encode(total)
            send(z_out.at[k - 1], z_in.at[k - 1], z_send, z_recv.at[k - 1], peer(0, k))

    def send_queries():
        for k in range(1, ny):
            send(q_hbm, qall.at[d], q_send, q_recv, peer_y(k, core))

        @pl.when(core == 1)
        def _():
            for k in range(ny):
                pl.semaphore_signal(in_core, inc=1, device_id=peer_y(k, 0), device_id_type=MESH)
                send(q_hbm, qall.at[d], q_send, q_recv, peer_y(k, 0))

    sent[0, 0:early] = encode(project(0))
    pl.semaphore_wait(barrier, len(partners) + core * ny + z)
    for i in range(early):
        send_far(i)
    for k in range(1, nz):
        @pl.when(z - k >= 0)
        def _(k=k):
            pl.semaphore_signal(in_z, inc=1, device_id=peer(0, nz - k), device_id_type=MESH)

    sent[0, early:] = encode(project(1))
    for i in range(early, half):
        send_far(i)
    sent[1, 0:early] = encode(project(2))
    send_raw(0)
    keep[0] = project(3)
    combine(0)
    for i in range(1, early):
        send_raw(i)
        combine(i)
    sent[1, early:] = encode(project(4))
    for i in range(early, half):
        send_raw(i)
        combine(i)
    send_queries()
    keep[1] = project(5)

    @pl.when(z + 1 < nz)
    def _():
        pl.semaphore_wait(in_z, nz - 1 - z)

    for i in range(half):
        total = reduce_x(i)

    @pl.when(core == 0)
    def _():
        pl.semaphore_wait(in_core, ny)
        for k in range(ny):
            send(q_hbm, qall.at[d], q_send, q_recv, peer_y(k, 1))

    for k in (k for pair in offsets for k in pair if k > 0):
        drain(z_in.at[k - 1], z_recv.at[k - 1])
        total += decode(z_in[k - 1])

    own_len.wait()
    live = (lax.broadcasted_iota(jnp.int32, (tokens, 2 * rank), 0) < len_ref[t]).astype(F32)
    lane = lax.broadcasted_iota(jnp.int32, (tokens, 2 * rank), 1)
    both = jnp.where(lane < rank, pltpu.roll(total, rank, 1), total)
    a_high, a_low = split(total * live)
    b_high, b_low = split(both)

    def outer(left_side, right_side):
        return lax.dot_general(left_side, right_side, (((0,), (0,)), ((), ())), preferred_element_type=F32)

    small[...] = (outer(a_high, b_high) + (outer(a_high, b_low) + outer(a_low, b_high)))[0:rank]
    pairs = rank // 2
    lane_half = lax.broadcasted_iota(jnp.int32, (pairs, 2 * rank), 1)
    example = jnp.where(lane_half < rank, small[pl.ds(0, pairs, stride=2), :], small[pl.ds(1, pairs, stride=2), :])
    exall[t] = example.astype(BF16)

    others = [(dx, dz) for dx in range(NX) for dz in range(nz) if (dx, dz) != (0, 0)]
    others.sort(key=lambda step: -(hops(step[0], NX) + hops(step[1], nz)))
    for dx, dz in others:
        send(exall.at[t], exall.at[t], ex_send, ex_recv, peer(dx, dz))
    count = exall.shape[0]

    own_q.wait()
    drain(qall.at[0:nd - 1], q_recv)
    rows = qall.shape[1]
    for k in range(0, nd, 2):
        qflat[k * rows:(k + 2) * rows, :] = jnp.concatenate([qall[k], qall[k + 1]], axis=0)

    drain(exall.at[0:count - 1], ex_recv)

    exwide[...] = exall[...].reshape(count * pairs, 2 * rank).astype(F32)
    flat = jnp.concatenate([exwide[pl.ds(r, count, stride=pairs), :] for r in range(pairs)], axis=1)
    out_ref[...] = lax.dot_general(
        flat.astype(BF16), qflat[...], (((1,), (1,)), ((), ())), preferred_element_type=F32
    )

    drain(sent, x_send)
    drain(z_out, z_send)
    drain(qall.at[0:nd - 1], q_send)
    drain(exall.at[0:count - 1], ex_send)


def solution(mesh):
    nt, nd = mesh.shape["tensor"], mesh.shape["dp"]
    nz = nt // NX
    half = nz // 2

    def body(inputs, out_grads, proj_in, proj_out, lengths, queries):
        seqs, tokens, feats = inputs.shape
        grads = out_grads.shape[2]
        rank = proj_in.shape[1]
        lanes = 2 * rank
        block = (tokens, lanes)
        dma = pltpu.SemaphoreType.DMA
        return pl.pallas_call(
            functools.partial(kernel, nz, nd),
            out_shape=jax.ShapeDtypeStruct((seqs, nd * queries.shape[0]), F32),
            in_specs=[pl.BlockSpec(memory_space=pltpu.HBM)] * 6,
            out_specs=pl.BlockSpec(memory_space=pltpu.VMEM),
            scratch_shapes=[
                pltpu.VMEM((seqs, tokens, feats + grads), BF16),
                pltpu.VMEM((lanes, feats + grads), BF16),
                pltpu.VMEM((feats + grads, lanes), BF16),
                pltpu.SMEM(lengths.shape, jnp.int32),
                pltpu.VMEM((3, half, 2) + block, BF16),
                pltpu.VMEM((2, half, 2) + block, F32),
                pltpu.VMEM((half, 2) + block, BF16),
                pltpu.VMEM((half, 2, 2) + block, BF16),
                pltpu.VMEM((nz - 1,) + block, BF16),
                pltpu.VMEM((nz - 1,) + block, BF16),
                pltpu.VMEM((nd,) + queries.shape, BF16),
                pltpu.VMEM((nd * queries.shape[0], queries.shape[1]), BF16),
                pltpu.VMEM((seqs, rank // 2, lanes), BF16),
                pltpu.VMEM((seqs * rank // 2, lanes), F32),
                pltpu.VMEM((rank, lanes), F32),
                dma((6,)),
            ] + [dma] * 3 + [pltpu.SemaphoreType.REGULAR] * 2 + [dma] * 4 + [dma((half, 2)), dma((half,)), dma((nz - 1,))] + [dma] * 2,
            compiler_params=pltpu.CompilerParams(
                collective_id=0, has_side_effects=True, vmem_limit_bytes=60 * 1024 * 1024
            ),
        )(inputs, out_grads, proj_in.T, proj_out.T, lengths, queries)

    return jax.shard_map(
        body,
        mesh=mesh,
        in_specs=(
            P("dp", None, "tensor"),
            P("dp", None, "tensor"),
            P("tensor", None),
            P("tensor", None),
            P("dp"),
            P(("tensor", "dp"), None),
        ),
        out_specs=P("dp", "tensor"),
        check_vma=False,
    )
```

```python
import functools

import jax
import jax.numpy as jnp
from jax import lax
from jax.experimental import pallas as pl
from jax.experimental.pallas import tpu as pltpu
from jax.sharding import PartitionSpec as P

MESH = pl.DeviceIdType.MESH
F32 = jnp.float32
BF16 = jnp.bfloat16
NX = 4


def encode(value):
    return (value * jnp.abs(value)).astype(BF16)


def decode(code):
    wide = code.astype(F32)
    root = jnp.sqrt(jnp.abs(wide))
    return jnp.where(wide < 0, -root, root)


def split(value):
    high = value.astype(BF16)
    return high, (value - high.astype(F32)).astype(BF16)


def hops(steps, size):
    return min(steps, size - steps)


def kernel(
    nz, nd,
    x_hbm, g_hbm, wi_hbm, wo_hbm, len_hbm, q_hbm, out_ref,
    acts, wt, w, len_ref, sent, keep, chain_in, final_in, z_out, z_in, qall, qflat, exall, exwide, small,
    load_sem, w_sem, len_sem, own_q_sem, in_core, in_z, x_send, z_send, q_send, ex_send, chain_recv, final_recv, z_recv, q_recv, ex_recv,
):
    half = nz // 2
    tokens, rank = x_hbm.shape[1], wi_hbm.shape[0]
    feats = x_hbm.shape[2]
    t = lax.axis_index("tensor")
    d = lax.axis_index("dp")
    x, z = t // nz, t % nz
    x_right, x_left, x_far = (x + 1) % NX, (x + NX - 1) % NX, (x + 2) % NX

    def peer(dx, dz):
        return {"tensor": ((x + dx) % NX) * nz + (z + dz) % nz, "dp": d}

    right, left = peer(1, 0), peer(NX - 1, 0)
    core, y, ny = d % 2, d // 2, nd // 2

    def peer_y(dy, side):
        return {"tensor": t, "dp": ((y + dy) % ny) * 2 + side}

    barrier = pltpu.get_barrier_semaphore()
    partners = [right, left]
    partners += [peer_y(k, core) for k in range(1, ny)]
    for partner in partners:
        pl.semaphore_signal(barrier, inc=1, device_id=partner, device_id_type=MESH)

    @pl.when(core == 0)
    def _():
        for k in range(ny):
            pl.semaphore_signal(barrier, inc=1, device_id=peer_y(k, 1), device_id_type=MESH)

    for k in range(1, nz):
        @pl.when(z + k < nz)
        def _(k=k):
            pl.semaphore_signal(barrier, inc=1, device_id=peer(0, k), device_id_type=MESH)

    offsets = [(half + i, half - 1 - i) for i in range(half)]
    chunks = [[], [], [], [], [], []]
    early = (half + 1) // 2
    for i, (even, odd) in enumerate(offsets):
        ze, zo = (z + even) % nz, (z + odd) % nz
        chunks[0 if i < early else 1] += [(x_far, ze), (x_far, zo)]
        chunks[2 if i < early else 4] += [(x_right, zo), (x_left, ze)]
        chunks[3] += [(x_right, ze), (x_left, zo)]
        chunks[5] += [(x, ze), (x, zo)]

    wt[...] = jnp.zeros_like(wt)
    pltpu.make_async_copy(wi_hbm, wt.at[0:rank, 0:feats], w_sem).start()
    pltpu.make_async_copy(wo_hbm, wt.at[rank:2 * rank, feats:], w_sem).start()
    starts = [0]
    for c, owners in enumerate(chunks):
        for k, (xd, zd) in enumerate(owners):
            s, slot = xd * nz + zd, starts[c] + k
            pltpu.make_async_copy(x_hbm.at[s], acts.at[slot, :, 0:feats], load_sem.at[c]).start()
            pltpu.make_async_copy(g_hbm.at[s], acts.at[slot, :, feats:], load_sem.at[c]).start()
        starts.append(starts[c] + len(owners))
    own_q = pltpu.make_async_copy(q_hbm, qall.at[d], own_q_sem)
    own_q.start()
    own_len = pltpu.make_async_copy(len_hbm, len_ref, len_sem)
    own_len.start()

    def drain(ref, sem):
        pltpu.make_async_copy(ref, ref, sem).wait()

    drain(wt.at[0:rank], w_sem)
    w[...] = wt[...].T

    def project(c):
        count = starts[c + 1] - starts[c]
        block = acts.at[starts[c]:starts[c + 1]]
        drain(block, load_sem.at[c])
        total = jnp.dot(
            block[:, :, 0:feats].reshape(count * tokens, feats), w[0:feats, :], preferred_element_type=F32
        )
        total += jnp.dot(
            block[:, :, feats:].reshape(count * tokens, block.shape[2] - feats), w[feats:, :], preferred_element_type=F32
        )
        return total.reshape(count // 2, 2, tokens, 2 * rank)

    def send(src, dst, send_sem, recv_sem, device):
        pltpu.make_async_remote_copy(
            src_ref=src, dst_ref=dst, send_sem=send_sem, recv_sem=recv_sem, device_id=device, device_id_type=MESH
        ).start()

    def send_far(i):
        for side, device in enumerate((right, left)):
            send(sent.at[0, i, side], chain_in.at[i, side], x_send, chain_recv.at[i, side], device)

    def send_raw(i):
        send(sent.at[1, i, 0], final_in.at[i, 1, 0], x_send, final_recv.at[i], right)
        send(sent.at[1, i, 1], final_in.at[i, 0, 1], x_send, final_recv.at[i], left)

    def combine(i):
        for side, device in enumerate((right, left)):
            drain(chain_in.at[i, side], chain_recv.at[i, side])
            sent[2, i, side] = encode(keep[0, i, side] + decode(chain_in[i, side]))
            send(sent.at[2, i, side], final_in.at[i, side, side], x_send, final_recv.at[i], device)

    def reduce_x(i):
        drain(final_in.at[i], final_recv.at[i])
        for parity, k in enumerate(offsets[i]):
            total = keep[1, i, parity] + (decode(final_in[i, parity, 0]) + decode(final_in[i, parity, 1]))
            if k == 0:
                return total
            z_out[k - 1] = encode(total)
            send(z_out.at[k - 1], z_in.at[k - 1], z_send, z_recv.at[k - 1], peer(0, k))

    def send_queries():
        for k in range(1, ny):
            send(q_hbm, qall.at[d], q_send, q_recv, peer_y(k, core))

        @pl.when(core == 1)
        def _():
            for k in range(ny):
                pl.semaphore_signal(in_core, inc=1, device_id=peer_y(k, 0), device_id_type=MESH)
                send(q_hbm, qall.at[d], q_send, q_recv, peer_y(k, 0))

    def place(c):
        if c == 0:
            sent[0, 0:early] = encode(project(c))
        elif c == 1:
            sent[0, early:] = encode(project(c))
        elif c == 2:
            sent[1, 0:early] = encode(project(c))
        elif c == 4:
            sent[1, early:] = encode(project(c))
        else:
            keep[(c - 3) // 2] = project(c)

    def block(c):
        pl.when(core >= 0)(lambda: place(c))

    block(0)
    pl.semaphore_wait(barrier, len(partners) + core * ny + z)
    for i in range(early):
        send_far(i)
    for k in range(1, nz):
        @pl.when(z - k >= 0)
        def _(k=k):
            pl.semaphore_signal(in_z, inc=1, device_id=peer(0, nz - k), device_id_type=MESH)

    block(1)
    for i in range(early, half):
        send_far(i)
    block(2)
    send_raw(0)
    block(3)
    combine(0)
    for i in range(1, early):
        send_raw(i)
        combine(i)
    block(4)
    for i in range(early, half):
        send_raw(i)
        combine(i)
    send_queries()
    block(5)

    @pl.when(z + 1 < nz)
    def _():
        pl.semaphore_wait(in_z, nz - 1 - z)

    for i in range(half):
        total = reduce_x(i)

    @pl.when(core == 0)
    def _():
        pl.semaphore_wait(in_core, ny)
        for k in range(ny):
            send(q_hbm, qall.at[d], q_send, q_recv, peer_y(k, 1))

    for k in (k for pair in offsets for k in pair if k > 0):
        drain(z_in.at[k - 1], z_recv.at[k - 1])
        total += decode(z_in[k - 1])

    own_len.wait()
    live = (lax.broadcasted_iota(jnp.int32, (tokens, 2 * rank), 0) < len_ref[t]).astype(F32)
    lane = lax.broadcasted_iota(jnp.int32, (tokens, 2 * rank), 1)
    both = jnp.where(lane < rank, pltpu.roll(total, rank, 1), total)
    a_high, a_low = split(total * live)
    b_high, b_low = split(both)

    def outer(left_side, right_side):
        return lax.dot_general(left_side, right_side, (((0,), (0,)), ((), ())), preferred_element_type=F32)

    small[...] = (outer(a_high, b_high) + (outer(a_high, b_low) + outer(a_low, b_high)))[0:rank]
    pairs = rank // 2
    lane_half = lax.broadcasted_iota(jnp.int32, (pairs, 2 * rank), 1)
    example = jnp.where(lane_half < rank, small[pl.ds(0, pairs, stride=2), :], small[pl.ds(1, pairs, stride=2), :])
    exall[t] = example.astype(BF16)

    others = [(dx, dz) for dx in range(NX) for dz in range(nz) if (dx, dz) != (0, 0)]
    others.sort(key=lambda step: -(hops(step[0], NX) + hops(step[1], nz)))
    for dx, dz in others:
        send(exall.at[t], exall.at[t], ex_send, ex_recv, peer(dx, dz))
    count = exall.shape[0]

    own_q.wait()
    drain(qall.at[0:nd - 1], q_recv)
    rows = qall.shape[1]
    for k in range(0, nd, 2):
        qflat[k * rows:(k + 2) * rows, :] = jnp.concatenate([qall[k], qall[k + 1]], axis=0)

    drain(exall.at[0:count - 1], ex_recv)

    exwide[...] = exall[...].reshape(count * pairs, 2 * rank).astype(F32)
    flat = jnp.concatenate([exwide[pl.ds(r, count, stride=pairs), :] for r in range(pairs)], axis=1)
    out_ref[...] = lax.dot_general(
        flat.astype(BF16), qflat[...], (((1,), (1,)), ((), ())), preferred_element_type=F32
    )

    drain(sent, x_send)
    drain(z_out, z_send)
    drain(qall.at[0:nd - 1], q_send)
    drain(exall.at[0:count - 1], ex_send)


def solution(mesh):
    nt, nd = mesh.shape["tensor"], mesh.shape["dp"]
    nz = nt // NX
    half = nz // 2

    def body(inputs, out_grads, proj_in, proj_out, lengths, queries):
        seqs, tokens, feats = inputs.shape
        grads = out_grads.shape[2]
        rank = proj_in.shape[1]
        lanes = 2 * rank
        block = (tokens, lanes)
        dma = pltpu.SemaphoreType.DMA
        return pl.pallas_call(
            functools.partial(kernel, nz, nd),
            out_shape=pltpu.VMEM((seqs, nd * queries.shape[0]), F32),
            in_specs=[pl.BlockSpec(memory_space=pltpu.HBM)] * 6,
            out_specs=pl.BlockSpec(memory_space=pltpu.VMEM),
            scratch_shapes=[
                pltpu.VMEM((seqs, tokens, feats + grads), BF16),
                pltpu.VMEM((lanes, feats + grads), BF16),
                pltpu.VMEM((feats + grads, lanes), BF16),
                pltpu.SMEM(lengths.shape, jnp.int32),
                pltpu.VMEM((3, half, 2) + block, BF16),
                pltpu.VMEM((2, half, 2) + block, F32),
                pltpu.VMEM((half, 2) + block, BF16),
                pltpu.VMEM((half, 2, 2) + block, BF16),
                pltpu.VMEM((nz - 1,) + block, BF16),
                pltpu.VMEM((nz - 1,) + block, BF16),
                pltpu.VMEM((nd,) + queries.shape, BF16),
                pltpu.VMEM((nd * queries.shape[0], queries.shape[1]), BF16),
                pltpu.VMEM((seqs, rank // 2, lanes), BF16),
                pltpu.VMEM((seqs * rank // 2, lanes), F32),
                pltpu.VMEM((rank, lanes), F32),
                dma((6,)),
            ] + [dma] * 3 + [pltpu.SemaphoreType.REGULAR] * 2 + [dma] * 4 + [dma((half, 2)), dma((half,)), dma((nz - 1,))] + [dma] * 2,
            compiler_params=pltpu.CompilerParams(
                collective_id=0, has_side_effects=True, vmem_limit_bytes=60 * 1024 * 1024
            ),
        )(*(
            pltpu.with_memory_space_constraint(operand, pltpu.HBM)
            for operand in (inputs, out_grads, proj_in.T, proj_out.T, lengths, queries)
        ))

    return jax.shard_map(
        body,
        mesh=mesh,
        in_specs=(
            P("dp", None, "tensor"),
            P("dp", None, "tensor"),
            P("tensor", None),
            P("tensor", None),
            P("dp"),
            P(("tensor", "dp"), None),
        ),
        out_specs=P("dp", "tensor"),
        check_vma=False,
    )
```

```python
import functools

import jax
import jax.numpy as jnp
from jax import lax
from jax.experimental import pallas as pl
from jax.experimental.pallas import tpu as pltpu
from jax.sharding import PartitionSpec as P

MESH = pl.DeviceIdType.MESH
F32 = jnp.float32
BF16 = jnp.bfloat16
NX = 4


def encode(value):
    return (value * jnp.abs(value)).astype(BF16)


def decode(code):
    wide = code.astype(F32)
    root = jnp.sqrt(jnp.abs(wide))
    return jnp.where(wide < 0, -root, root)


def split(value):
    high = value.astype(BF16)
    return high, (value - high.astype(F32)).astype(BF16)


def hops(steps, size):
    return min(steps, size - steps)


def kernel(
    nz, nd,
    x_hbm, g_hbm, wi_hbm, wo_hbm, len_hbm, q_hbm, out_ref,
    acts, wt, w, len_ref, sent, keep, chain_in, final_in, z_out, z_in, qall, qflat, exall, exwide, small,
    load_sem, w_sem, len_sem, own_q_sem, in_z, x_send, z_send, q_send, ex_send, chain_recv, final_recv, z_recv, ex_recv, q_recv,
):
    half = nz // 2
    tokens, rank = x_hbm.shape[1], wi_hbm.shape[0]
    feats = x_hbm.shape[2]
    t = lax.axis_index("tensor")
    d = lax.axis_index("dp")
    x, z = t // nz, t % nz
    x_right, x_left, x_far = (x + 1) % NX, (x + NX - 1) % NX, (x + 2) % NX

    def peer(dx, dz):
        return {"tensor": ((x + dx) % NX) * nz + (z + dz) % nz, "dp": d}

    right, left = peer(1, 0), peer(NX - 1, 0)
    core, y, ny = d % 2, d // 2, nd // 2

    def peer_y(dy, side):
        return {"tensor": t, "dp": ((y + dy) % ny) * 2 + side}

    near_y = sorted({1, ny - 1} - {0}) if ny > 1 else []
    far_y = [k for k in range(1, ny) if k not in near_y]
    barrier = pltpu.get_barrier_semaphore()
    partners = [right, left]
    partners += [peer_y(k, core) for k in near_y]
    for partner in partners:
        pl.semaphore_signal(barrier, inc=1, device_id=partner, device_id_type=MESH)

    @pl.when(core == 0)
    def _():
        pl.semaphore_signal(barrier, inc=1, device_id=peer_y(0, 1), device_id_type=MESH)

    for k in range(1, nz):
        @pl.when(z + k < nz)
        def _(k=k):
            pl.semaphore_signal(barrier, inc=1, device_id=peer(0, k), device_id_type=MESH)

    offsets = [(half + i, half - 1 - i) for i in range(half)]
    chunks = [[], [], [], [], [], []]
    early = (half + 1) // 2
    first = max(half // 4, 1)
    for i, (even, odd) in enumerate(offsets):
        ze, zo = (z + even) % nz, (z + odd) % nz
        chunks[0 if i < first else 1] += [(x_far, ze), (x_far, zo)]
        chunks[2 if i < early else 4] += [(x_right, zo), (x_left, ze)]
        chunks[3] += [(x_right, ze), (x_left, zo)]
        chunks[5] += [(x, ze), (x, zo)]

    wt[...] = jnp.zeros_like(wt)
    pltpu.make_async_copy(wi_hbm, wt.at[0:rank, 0:feats], w_sem).start()
    pltpu.make_async_copy(wo_hbm, wt.at[rank:2 * rank, feats:], w_sem).start()
    starts = [0]
    for c, owners in enumerate(chunks):
        for k, (xd, zd) in enumerate(owners):
            s, slot = xd * nz + zd, starts[c] + k
            pltpu.make_async_copy(x_hbm.at[s], acts.at[slot, :, 0:feats], load_sem.at[c]).start()
            pltpu.make_async_copy(g_hbm.at[s], acts.at[slot, :, feats:], load_sem.at[c]).start()
        starts.append(starts[c] + len(owners))
    own_q = pltpu.make_async_copy(q_hbm, qall.at[d], own_q_sem)
    own_q.start()
    own_len = pltpu.make_async_copy(len_hbm, len_ref, len_sem)
    own_len.start()

    def drain(ref, sem):
        pltpu.make_async_copy(ref, ref, sem).wait()

    drain(wt.at[0:rank], w_sem)
    w[...] = wt[...].T

    def project(c):
        count = starts[c + 1] - starts[c]
        block = acts.at[starts[c]:starts[c + 1]]
        drain(block, load_sem.at[c])
        total = jnp.dot(
            block[:, :, 0:feats].reshape(count * tokens, feats), w[0:feats, :], preferred_element_type=F32
        )
        total += jnp.dot(
            block[:, :, feats:].reshape(count * tokens, block.shape[2] - feats), w[feats:, :], preferred_element_type=F32
        )
        return total.reshape(count // 2, 2, tokens, 2 * rank)

    def send(src, dst, send_sem, recv_sem, device):
        pltpu.make_async_remote_copy(
            src_ref=src, dst_ref=dst, send_sem=send_sem, recv_sem=recv_sem, device_id=device, device_id_type=MESH
        ).start()

    def send_far(i):
        for side, device in enumerate((right, left)):
            send(sent.at[0, i, side], chain_in.at[i, side], x_send, chain_recv.at[i, side], device)

    def send_raw(i):
        send(sent.at[1, i, 0], final_in.at[i, 1, 0], x_send, final_recv.at[i], right)
        send(sent.at[1, i, 1], final_in.at[i, 0, 1], x_send, final_recv.at[i], left)

    def combine(i):
        for side, device in enumerate((right, left)):
            drain(chain_in.at[i, side], chain_recv.at[i, side])
            sent[2, i, side] = encode(keep[0, i, side] + decode(chain_in[i, side]))
            send(sent.at[2, i, side], final_in.at[i, side, side], x_send, final_recv.at[i], device)

    def reduce_x(i):
        drain(final_in.at[i], final_recv.at[i])
        for parity, k in enumerate(offsets[i]):
            total = keep[1, i, parity] + (decode(final_in[i, parity, 0]) + decode(final_in[i, parity, 1]))
            if k == 0:
                return total
            z_out[k - 1] = encode(total)
            send(z_out.at[k - 1], z_in.at[k - 1], z_send, z_recv.at[k - 1], peer(0, k))

    def send_query(k, side):
        send(q_hbm, qall.at[d], q_send, q_recv.at[(core + side) % 2, k], peer_y(k, side))

    def take_query(k, side):
        drain(qall.at[0], q_recv.at[(core + side) % 2, k])

    def on(side):
        return pl.when(core == side)

    def first_queries():
        for k in near_y:
            send_query(k, core)
        on(1)(lambda: send_query(0, 0))

    def second_queries():
        for k in near_y:
            take_query(k, core)
        for k in far_y:
            send_query(k, core)

        @on(1)
        def _():
            for k in near_y:
                send_query(k, 0)

    def third_queries():
        for k in far_y:
            take_query(k, core)

        @on(1)
        def _():
            for k in far_y:
                send_query(k, 0)

        @on(0)
        def _():
            for k in [0] + near_y:
                take_query(k, 1)
                send_query((ny - k) % ny, 1)

    def last_queries():
        @on(0)
        def _():
            for k in far_y:
                take_query(k, 1)
                send_query((ny - k) % ny, 1)

        @on(1)
        def _():
            for k in [0] + near_y + far_y:
                take_query(k, 0)

    def place(c):
        if c == 0:
            sent[0, 0:first] = encode(project(c))
        elif c == 1:
            sent[0, first:] = encode(project(c))
        elif c == 2:
            sent[1, 0:early] = encode(project(c))
        elif c == 4:
            sent[1, early:] = encode(project(c))
        else:
            keep[(c - 3) // 2] = project(c)

    def block(c):
        pl.when(core >= 0)(lambda: place(c))

    block(0)
    pl.semaphore_wait(barrier, len(partners) + core + z)
    for i in range(first):
        send_far(i)
    for k in range(1, nz):
        @pl.when(z - k >= 0)
        def _(k=k):
            pl.semaphore_signal(in_z, inc=1, device_id=peer(0, nz - k), device_id_type=MESH)

    block(1)
    for i in range(first, half):
        send_far(i)
    block(2)
    send_raw(0)
    first_queries()
    block(3)
    combine(0)
    for i in range(1, early):
        send_raw(i)
        combine(i)
    block(4)
    for i in range(early, half):
        send_raw(i)
        combine(i)
    second_queries()
    block(5)

    @pl.when(z + 1 < nz)
    def _():
        pl.semaphore_wait(in_z, nz - 1 - z)

    for i in range(half):
        total = reduce_x(i)

    third_queries()
    for k in (k for pair in offsets for k in pair if k > 0):
        drain(z_in.at[k - 1], z_recv.at[k - 1])
        total += decode(z_in[k - 1])

    own_len.wait()
    live = (lax.broadcasted_iota(jnp.int32, (tokens, 2 * rank), 0) < len_ref[t]).astype(F32)
    lane = lax.broadcasted_iota(jnp.int32, (tokens, 2 * rank), 1)
    both = jnp.where(lane < rank, pltpu.roll(total, rank, 1), total)
    a_high, a_low = split(total * live)
    b_high, b_low = split(both)

    def outer(left_side, right_side):
        return lax.dot_general(left_side, right_side, (((0,), (0,)), ((), ())), preferred_element_type=F32)

    small[...] = (outer(a_high, b_high) + (outer(a_high, b_low) + outer(a_low, b_high)))[0:rank]
    pairs = rank // 2
    lane_half = lax.broadcasted_iota(jnp.int32, (pairs, 2 * rank), 1)
    example = jnp.where(lane_half < rank, small[pl.ds(0, pairs, stride=2), :], small[pl.ds(1, pairs, stride=2), :])
    exall[t] = example.astype(BF16)

    others = [(dx, dz) for dx in range(NX) for dz in range(nz) if (dx, dz) != (0, 0)]
    others.sort(key=lambda step: -(hops(step[0], NX) + hops(step[1], nz)))
    for dx, dz in others:
        send(exall.at[t], exall.at[t], ex_send, ex_recv, peer(dx, dz))
    count = exall.shape[0]

    own_q.wait()
    last_queries()
    rows = qall.shape[1]
    for k in range(0, nd, 2):
        qflat[k * rows:(k + 2) * rows, :] = jnp.concatenate([qall[k], qall[k + 1]], axis=0)

    drain(exall.at[0:count - 1], ex_recv)

    exwide[...] = exall[...].reshape(count * pairs, 2 * rank).astype(F32)
    flat = jnp.concatenate([exwide[pl.ds(r, count, stride=pairs), :] for r in range(pairs)], axis=1)
    out_ref[...] = lax.dot_general(
        flat.astype(BF16), qflat[...], (((1,), (1,)), ((), ())), preferred_element_type=F32
    )

    drain(sent, x_send)
    drain(z_out, z_send)
    drain(qall.at[0:nd - 1], q_send)
    drain(exall.at[0:count - 1], ex_send)


def solution(mesh):
    nt, nd = mesh.shape["tensor"], mesh.shape["dp"]
    nz = nt // NX
    half = nz // 2

    def body(inputs, out_grads, proj_in, proj_out, lengths, queries):
        seqs, tokens, feats = inputs.shape
        grads = out_grads.shape[2]
        rank = proj_in.shape[1]
        lanes = 2 * rank
        block = (tokens, lanes)
        dma = pltpu.SemaphoreType.DMA
        return pl.pallas_call(
            functools.partial(kernel, nz, nd),
            out_shape=pltpu.VMEM((seqs, nd * queries.shape[0]), F32),
            in_specs=[pl.BlockSpec(memory_space=pltpu.HBM)] * 6,
            out_specs=pl.BlockSpec(memory_space=pltpu.VMEM),
            scratch_shapes=[
                pltpu.VMEM((seqs, tokens, feats + grads), BF16),
                pltpu.VMEM((lanes, feats + grads), BF16),
                pltpu.VMEM((feats + grads, lanes), BF16),
                pltpu.SMEM(lengths.shape, jnp.int32),
                pltpu.VMEM((3, half, 2) + block, BF16),
                pltpu.VMEM((2, half, 2) + block, F32),
                pltpu.VMEM((half, 2) + block, BF16),
                pltpu.VMEM((half, 2, 2) + block, BF16),
                pltpu.VMEM((nz - 1,) + block, BF16),
                pltpu.VMEM((nz - 1,) + block, BF16),
                pltpu.VMEM((nd,) + queries.shape, BF16),
                pltpu.VMEM((nd * queries.shape[0], queries.shape[1]), BF16),
                pltpu.VMEM((seqs, rank // 2, lanes), BF16),
                pltpu.VMEM((seqs * rank // 2, lanes), F32),
                pltpu.VMEM((rank, lanes), F32),
                dma((6,)),
            ] + [dma] * 3 + [pltpu.SemaphoreType.REGULAR] + [dma] * 4 + [dma((half, 2)), dma((half,)), dma((nz - 1,))] + [dma, dma((2, nd // 2))],
            compiler_params=pltpu.CompilerParams(
                collective_id=0, has_side_effects=True, vmem_limit_bytes=60 * 1024 * 1024
            ),
        )(*(
            pltpu.with_memory_space_constraint(operand, pltpu.HBM)
            for operand in (inputs, out_grads, proj_in.T, proj_out.T, lengths, queries)
        ))

    return jax.shard_map(
        body,
        mesh=mesh,
        in_specs=(
            P("dp", None, "tensor"),
            P("dp", None, "tensor"),
            P("tensor", None),
            P("tensor", None),
            P("dp"),
            P(("tensor", "dp"), None),
        ),
        out_specs=P("dp", "tensor"),
        check_vma=False,
    )
```

```python
import functools

import jax
import jax.numpy as jnp
from jax import lax
from jax.experimental import pallas as pl
from jax.experimental.pallas import tpu as pltpu
from jax.sharding import PartitionSpec as P

MESH = pl.DeviceIdType.MESH
F32 = jnp.float32
BF16 = jnp.bfloat16
NX = 4


def encode(value):
    return (value * jnp.abs(value)).astype(BF16)


def decode(code):
    wide = code.astype(F32)
    root = jnp.sqrt(jnp.abs(wide))
    return jnp.where(wide < 0, -root, root)


def split(value):
    high = value.astype(BF16)
    return high, (value - high.astype(F32)).astype(BF16)


def hops(steps, size):
    return min(steps, size - steps)


def kernel(
    nz, nd,
    x_hbm, g_hbm, wi_hbm, wo_hbm, len_hbm, q_hbm, out_ref,
    acts, wt, w, len_ref, sent, keep, chain_in, final_in, z_out, z_in, qall, qflat, exall, exwide, small,
    load_sem, w_sem, len_sem, own_q_sem, in_z, x_send, z_send, q_send, ex_send, chain_recv, final_recv, z_recv, ex_recv, q_recv,
):
    half = nz // 2
    tokens, rank = x_hbm.shape[1], wi_hbm.shape[0]
    feats = x_hbm.shape[2]
    t = lax.axis_index("tensor")
    d = lax.axis_index("dp")
    x, z = t // nz, t % nz
    x_right, x_left, x_far = (x + 1) % NX, (x + NX - 1) % NX, (x + 2) % NX

    def peer(dx, dz):
        return {"tensor": ((x + dx) % NX) * nz + (z + dz) % nz, "dp": d}

    right, left = peer(1, 0), peer(NX - 1, 0)
    core, y, ny = d % 2, d // 2, nd // 2

    def peer_y(dy, side):
        return {"tensor": t, "dp": ((y + dy) % ny) * 2 + side}

    near_y = sorted({1, ny - 1} - {0}) if ny > 1 else []
    far_y = [k for k in range(1, ny) if k not in near_y]
    barrier = pltpu.get_barrier_semaphore()
    partners = [right, left]
    partners += [peer_y(k, core) for k in near_y]
    for partner in partners:
        pl.semaphore_signal(barrier, inc=1, device_id=partner, device_id_type=MESH)

    @pl.when(core == 0)
    def _():
        pl.semaphore_signal(barrier, inc=1, device_id=peer_y(0, 1), device_id_type=MESH)

    for k in range(1, nz):
        @pl.when(z + k < nz)
        def _(k=k):
            pl.semaphore_signal(barrier, inc=1, device_id=peer(0, k), device_id_type=MESH)

    offsets = [(half + i, half - 1 - i) for i in range(half)]
    chunks = [[], [], [], [], [], []]
    early = (half + 1) // 2
    first = max(half // 4, 1)
    for i, (even, odd) in enumerate(offsets):
        ze, zo = (z + even) % nz, (z + odd) % nz
        chunks[0 if i < first else 1] += [(x_far, ze), (x_far, zo)]
        chunks[2 if i < early else 4] += [(x_right, zo), (x_left, ze)]
        chunks[3] += [(x_right, ze), (x_left, zo)]
        chunks[5] += [(x, ze), (x, zo)]

    starts = [0]
    for owners in chunks:
        starts.append(starts[-1] + len(owners))

    def load(c):
        for k, (xd, zd) in enumerate(chunks[c]):
            s, slot = xd * nz + zd, starts[c] + k
            pltpu.make_async_copy(x_hbm.at[s], acts.at[slot, :, 0:feats], load_sem.at[c]).start()
            pltpu.make_async_copy(g_hbm.at[s], acts.at[slot, :, feats:], load_sem.at[c]).start()

    own_q = pltpu.make_async_copy(q_hbm, qall.at[d], own_q_sem)
    own_len = pltpu.make_async_copy(len_hbm, len_ref, len_sem)
    wt[...] = jnp.zeros_like(wt)
    pltpu.make_async_copy(wi_hbm, wt.at[0:rank, 0:feats], w_sem).start()
    pltpu.make_async_copy(wo_hbm, wt.at[rank:2 * rank, feats:], w_sem).start()
    load(0)

    def drain(ref, sem):
        pltpu.make_async_copy(ref, ref, sem).wait()

    drain(wt.at[0:rank], w_sem)
    for c in range(1, len(chunks)):
        load(c)
    own_q.start()
    own_len.start()
    w[...] = wt[...].T

    def project(c):
        count = starts[c + 1] - starts[c]
        block = acts.at[starts[c]:starts[c + 1]]
        drain(block, load_sem.at[c])
        total = jnp.dot(
            block[:, :, 0:feats].reshape(count * tokens, feats), w[0:feats, :], preferred_element_type=F32
        )
        total += jnp.dot(
            block[:, :, feats:].reshape(count * tokens, block.shape[2] - feats), w[feats:, :], preferred_element_type=F32
        )
        return total.reshape(count // 2, 2, tokens, 2 * rank)

    def send(src, dst, send_sem, recv_sem, device):
        pltpu.make_async_remote_copy(
            src_ref=src, dst_ref=dst, send_sem=send_sem, recv_sem=recv_sem, device_id=device, device_id_type=MESH
        ).start()

    def send_far(i):
        for side, device in enumerate((right, left)):
            send(sent.at[0, i, side], chain_in.at[i, side], x_send, chain_recv.at[i, side], device)

    def send_raw(i):
        send(sent.at[1, i, 0], final_in.at[i, 1, 0], x_send, final_recv.at[i], right)
        send(sent.at[1, i, 1], final_in.at[i, 0, 1], x_send, final_recv.at[i], left)

    def combine(i):
        for side, device in enumerate((right, left)):
            drain(chain_in.at[i, side], chain_recv.at[i, side])
            sent[2, i, side] = encode(keep[0, i, side] + decode(chain_in[i, side]))
            send(sent.at[2, i, side], final_in.at[i, side, side], x_send, final_recv.at[i], device)

    def reduce_x(i):
        drain(final_in.at[i], final_recv.at[i])
        for parity, k in enumerate(offsets[i]):
            total = keep[1, i, parity] + (decode(final_in[i, parity, 0]) + decode(final_in[i, parity, 1]))
            if k == 0:
                return total
            z_out[k - 1] = encode(total)
            send(z_out.at[k - 1], z_in.at[k - 1], z_send, z_recv.at[k - 1], peer(0, k))

    def send_query(k, side):
        send(q_hbm, qall.at[d], q_send, q_recv.at[(core + side) % 2, k], peer_y(k, side))

    def take_query(k, side):
        drain(qall.at[0], q_recv.at[(core + side) % 2, k])

    def on(side):
        return pl.when(core == side)

    def first_queries():
        for k in near_y:
            send_query(k, core)
        on(1)(lambda: send_query(0, 0))

    def second_queries():
        for k in near_y:
            take_query(k, core)
        for k in far_y:
            send_query(k, core)

        @on(1)
        def _():
            for k in near_y:
                send_query(k, 0)

    def third_queries():
        for k in far_y:
            take_query(k, core)

        @on(1)
        def _():
            for k in far_y:
                send_query(k, 0)

        @on(0)
        def _():
            for k in [0] + near_y:
                take_query(k, 1)
                send_query((ny - k) % ny, 1)

    def last_queries():
        @on(0)
        def _():
            for k in far_y:
                take_query(k, 1)
                send_query((ny - k) % ny, 1)

        @on(1)
        def _():
            for k in [0] + near_y + far_y:
                take_query(k, 0)

    def place(c):
        if c == 0:
            sent[0, 0:first] = encode(project(c))
        elif c == 1:
            sent[0, first:] = encode(project(c))
        elif c == 2:
            sent[1, 0:early] = encode(project(c))
        elif c == 4:
            sent[1, early:] = encode(project(c))
        else:
            keep[(c - 3) // 2] = project(c)

    def block(c):
        pl.when(core >= 0)(lambda: place(c))

    block(0)
    pl.semaphore_wait(barrier, len(partners) + core + z)
    for i in range(first):
        send_far(i)
    for k in range(1, nz):
        @pl.when(z - k >= 0)
        def _(k=k):
            pl.semaphore_signal(in_z, inc=1, device_id=peer(0, nz - k), device_id_type=MESH)

    block(1)
    for i in range(first, half):
        send_far(i)
    block(2)
    send_raw(0)
    first_queries()
    block(3)
    combine(0)
    for i in range(1, early):
        send_raw(i)
        combine(i)
    block(4)
    for i in range(early, half):
        send_raw(i)
        combine(i)
    second_queries()
    block(5)

    @pl.when(z + 1 < nz)
    def _():
        pl.semaphore_wait(in_z, nz - 1 - z)

    for i in range(half):
        total = reduce_x(i)

    third_queries()
    for k in (k for pair in offsets for k in pair if k > 0):
        drain(z_in.at[k - 1], z_recv.at[k - 1])
        total += decode(z_in[k - 1])

    own_len.wait()
    live = (lax.broadcasted_iota(jnp.int32, (tokens, 2 * rank), 0) < len_ref[t]).astype(F32)
    lane = lax.broadcasted_iota(jnp.int32, (tokens, 2 * rank), 1)
    both = jnp.where(lane < rank, pltpu.roll(total, rank, 1), total)
    a_high, a_low = split(total * live)
    b_high, b_low = split(both)

    def outer(left_side, right_side):
        return lax.dot_general(left_side, right_side, (((0,), (0,)), ((), ())), preferred_element_type=F32)

    small[...] = (outer(a_high, b_high) + (outer(a_high, b_low) + outer(a_low, b_high)))[0:rank]
    pairs = rank // 2
    lane_half = lax.broadcasted_iota(jnp.int32, (pairs, 2 * rank), 1)
    example = jnp.where(lane_half < rank, small[pl.ds(0, pairs, stride=2), :], small[pl.ds(1, pairs, stride=2), :])
    exall[t] = example.astype(BF16)

    others = [(dx, dz) for dx in range(NX) for dz in range(nz) if (dx, dz) != (0, 0)]
    others.sort(key=lambda step: -(hops(step[0], NX) + hops(step[1], nz)))
    for dx, dz in others:
        send(exall.at[t], exall.at[t], ex_send, ex_recv, peer(dx, dz))
    count = exall.shape[0]

    own_q.wait()
    last_queries()
    rows = qall.shape[1]
    for k in range(0, nd, 2):
        qflat[k * rows:(k + 2) * rows, :] = jnp.concatenate([qall[k], qall[k + 1]], axis=0)

    drain(exall.at[0:count - 1], ex_recv)

    exwide[...] = exall[...].reshape(count * pairs, 2 * rank).astype(F32)
    flat = jnp.concatenate([exwide[pl.ds(r, count, stride=pairs), :] for r in range(pairs)], axis=1)
    out_ref[...] = lax.dot_general(
        flat.astype(BF16), qflat[...], (((1,), (1,)), ((), ())), preferred_element_type=F32
    )

    drain(sent, x_send)
    drain(z_out, z_send)
    drain(qall.at[0:nd - 1], q_send)
    drain(exall.at[0:count - 1], ex_send)


def solution(mesh):
    nt, nd = mesh.shape["tensor"], mesh.shape["dp"]
    nz = nt // NX
    half = nz // 2

    def body(inputs, out_grads, proj_in, proj_out, lengths, queries):
        seqs, tokens, feats = inputs.shape
        grads = out_grads.shape[2]
        rank = proj_in.shape[1]
        lanes = 2 * rank
        block = (tokens, lanes)
        dma = pltpu.SemaphoreType.DMA
        return pl.pallas_call(
            functools.partial(kernel, nz, nd),
            out_shape=pltpu.VMEM((seqs, nd * queries.shape[0]), F32),
            in_specs=[pl.BlockSpec(memory_space=pltpu.HBM)] * 6,
            out_specs=pl.BlockSpec(memory_space=pltpu.VMEM),
            scratch_shapes=[
                pltpu.VMEM((seqs, tokens, feats + grads), BF16),
                pltpu.VMEM((lanes, feats + grads), BF16),
                pltpu.VMEM((feats + grads, lanes), BF16),
                pltpu.SMEM(lengths.shape, jnp.int32),
                pltpu.VMEM((3, half, 2) + block, BF16),
                pltpu.VMEM((2, half, 2) + block, F32),
                pltpu.VMEM((half, 2) + block, BF16),
                pltpu.VMEM((half, 2, 2) + block, BF16),
                pltpu.VMEM((nz - 1,) + block, BF16),
                pltpu.VMEM((nz - 1,) + block, BF16),
                pltpu.VMEM((nd,) + queries.shape, BF16),
                pltpu.VMEM((nd * queries.shape[0], queries.shape[1]), BF16),
                pltpu.VMEM((seqs, rank // 2, lanes), BF16),
                pltpu.VMEM((seqs * rank // 2, lanes), F32),
                pltpu.VMEM((rank, lanes), F32),
                dma((6,)),
            ] + [dma] * 3 + [pltpu.SemaphoreType.REGULAR] + [dma] * 4 + [dma((half, 2)), dma((half,)), dma((nz - 1,))] + [dma, dma((2, nd // 2))],
            compiler_params=pltpu.CompilerParams(
                collective_id=0, has_side_effects=True, vmem_limit_bytes=60 * 1024 * 1024
            ),
        )(*(
            pltpu.with_memory_space_constraint(operand, pltpu.HBM)
            for operand in (inputs, out_grads, proj_in.T, proj_out.T, lengths, queries)
        ))

    return jax.shard_map(
        body,
        mesh=mesh,
        in_specs=(
            P("dp", None, "tensor"),
            P("dp", None, "tensor"),
            P("tensor", None),
            P("tensor", None),
            P("dp"),
            P(("tensor", "dp"), None),
        ),
        out_specs=P("dp", "tensor"),
        check_vma=False,
    )
```

```python
import functools

import jax
import jax.numpy as jnp
from jax import lax
from jax.experimental import pallas as pl
from jax.experimental.pallas import tpu as pltpu
from jax.sharding import PartitionSpec as P

MESH = pl.DeviceIdType.MESH
F32 = jnp.float32
BF16 = jnp.bfloat16
NX = 4


SCALE = 2.0**50


def encode(value):
    scaled = value * SCALE
    return (scaled * jnp.abs(scaled)).astype(BF16)


def decode(code):
    wide = code.astype(F32)
    root = jnp.sqrt(jnp.abs(wide)) * (1.0 / SCALE)
    return jnp.where(wide < 0, -root, root)


def split(value):
    high = value.astype(BF16)
    return high, (value - high.astype(F32)).astype(BF16)


def hops(steps, size):
    return min(steps, size - steps)


def kernel(
    nz, nd,
    x_hbm, g_hbm, wi_hbm, wo_hbm, len_hbm, q_hbm, out_ref,
    acts, wt, w, len_ref, sent, keep, chain_in, final_in, z_out, z_in, qall, qflat, exall, exwide, small,
    load_sem, w_sem, len_sem, own_q_sem, in_z, x_send, z_send, q_send, ex_send, chain_recv, final_recv, z_recv, ex_recv, q_recv,
):
    half = nz // 2
    tokens, rank = x_hbm.shape[1], wi_hbm.shape[0]
    feats = x_hbm.shape[2]
    t = lax.axis_index("tensor")
    d = lax.axis_index("dp")
    x, z = t // nz, t % nz
    x_right, x_left, x_far = (x + 1) % NX, (x + NX - 1) % NX, (x + 2) % NX

    def peer(dx, dz):
        return {"tensor": ((x + dx) % NX) * nz + (z + dz) % nz, "dp": d}

    right, left = peer(1, 0), peer(NX - 1, 0)
    core, y, ny = d % 2, d // 2, nd // 2

    def peer_y(dy, side):
        return {"tensor": t, "dp": ((y + dy) % ny) * 2 + side}

    near_y = sorted({1, ny - 1} - {0}) if ny > 1 else []
    far_y = [k for k in range(1, ny) if k not in near_y]
    barrier = pltpu.get_barrier_semaphore()
    partners = [right, left]
    partners += [peer_y(k, core) for k in near_y]
    for partner in partners:
        pl.semaphore_signal(barrier, inc=1, device_id=partner, device_id_type=MESH)

    @pl.when(core == 0)
    def _():
        pl.semaphore_signal(barrier, inc=1, device_id=peer_y(0, 1), device_id_type=MESH)

    for k in range(1, nz):
        @pl.when(z + k < nz)
        def _(k=k):
            pl.semaphore_signal(barrier, inc=1, device_id=peer(0, k), device_id_type=MESH)

    offsets = [(half + i, half - 1 - i) for i in range(half)]
    chunks = [[], [], [], [], [], []]
    early = (half + 1) // 2
    first = max(half // 4, 1)
    for i, (even, odd) in enumerate(offsets):
        ze, zo = (z + even) % nz, (z + odd) % nz
        chunks[0 if i < first else 1] += [(x_far, ze), (x_far, zo)]
        chunks[2 if i < early else 4] += [(x_right, zo), (x_left, ze)]
        chunks[3] += [(x_right, ze), (x_left, zo)]
        chunks[5] += [(x, ze), (x, zo)]

    starts = [0]
    for owners in chunks:
        starts.append(starts[-1] + len(owners))

    def load(c):
        for k, (xd, zd) in enumerate(chunks[c]):
            s, slot = xd * nz + zd, starts[c] + k
            pltpu.make_async_copy(x_hbm.at[s], acts.at[slot, :, 0:feats], load_sem.at[c]).start()
            pltpu.make_async_copy(g_hbm.at[s], acts.at[slot, :, feats:], load_sem.at[c]).start()

    own_q = pltpu.make_async_copy(q_hbm, qall.at[d], own_q_sem)
    own_len = pltpu.make_async_copy(len_hbm, len_ref, len_sem)
    wt[...] = jnp.zeros_like(wt)
    pltpu.make_async_copy(wi_hbm, wt.at[0:rank, 0:feats], w_sem).start()
    pltpu.make_async_copy(wo_hbm, wt.at[rank:2 * rank, feats:], w_sem).start()
    load(0)

    def drain(ref, sem):
        pltpu.make_async_copy(ref, ref, sem).wait()

    drain(wt.at[0:rank], w_sem)
    for c in range(1, len(chunks)):
        load(c)
    own_q.start()
    own_len.start()
    w[...] = wt[...].T

    def project(c):
        count = starts[c + 1] - starts[c]
        block = acts.at[starts[c]:starts[c + 1]]
        drain(block, load_sem.at[c])
        total = jnp.dot(
            block[:, :, 0:feats].reshape(count * tokens, feats), w[0:feats, :], preferred_element_type=F32
        )
        total += jnp.dot(
            block[:, :, feats:].reshape(count * tokens, block.shape[2] - feats), w[feats:, :], preferred_element_type=F32
        )
        return total.reshape(count // 2, 2, tokens, 2 * rank)

    def send(src, dst, send_sem, recv_sem, device):
        pltpu.make_async_remote_copy(
            src_ref=src, dst_ref=dst, send_sem=send_sem, recv_sem=recv_sem, device_id=device, device_id_type=MESH
        ).start()

    def send_far(i):
        for side, device in enumerate((right, left)):
            send(sent.at[0, i, side], chain_in.at[i, side], x_send, chain_recv.at[i, side], device)

    def send_raw(i):
        send(sent.at[1, i, 0], final_in.at[i, 1, 0], x_send, final_recv.at[i], right)
        send(sent.at[1, i, 1], final_in.at[i, 0, 1], x_send, final_recv.at[i], left)

    def combine(i):
        for side, device in enumerate((right, left)):
            drain(chain_in.at[i, side], chain_recv.at[i, side])
            sent[2, i, side] = encode(keep[0, i, side] + decode(chain_in[i, side]))
            send(sent.at[2, i, side], final_in.at[i, side, side], x_send, final_recv.at[i], device)

    def reduce_x(i):
        drain(final_in.at[i], final_recv.at[i])
        for parity, k in enumerate(offsets[i]):
            total = keep[1, i, parity] + (decode(final_in[i, parity, 0]) + decode(final_in[i, parity, 1]))
            if k == 0:
                return total
            z_out[k - 1] = encode(total)
            send(z_out.at[k - 1], z_in.at[k - 1], z_send, z_recv.at[k - 1], peer(0, k))

    def send_query(k, side):
        send(q_hbm, qall.at[d], q_send, q_recv.at[(core + side) % 2, k], peer_y(k, side))

    def take_query(k, side):
        drain(qall.at[0], q_recv.at[(core + side) % 2, k])

    def on(side):
        return pl.when(core == side)

    def first_queries():
        for k in near_y:
            send_query(k, core)
        on(1)(lambda: send_query(0, 0))

    def second_queries():
        for k in near_y:
            take_query(k, core)
        for k in far_y:
            send_query(k, core)

        @on(1)
        def _():
            for k in near_y:
                send_query(k, 0)

    def third_queries():
        for k in far_y:
            take_query(k, core)

        @on(1)
        def _():
            for k in far_y:
                send_query(k, 0)

        @on(0)
        def _():
            for k in [0] + near_y:
                take_query(k, 1)
                send_query((ny - k) % ny, 1)

    def last_queries():
        @on(0)
        def _():
            for k in far_y:
                take_query(k, 1)
                send_query((ny - k) % ny, 1)

        @on(1)
        def _():
            for k in [0] + near_y + far_y:
                take_query(k, 0)

    def place(c):
        if c == 0:
            sent[0, 0:first] = encode(project(c))
        elif c == 1:
            sent[0, first:] = encode(project(c))
        elif c == 2:
            sent[1, 0:early] = encode(project(c))
        elif c == 4:
            sent[1, early:] = encode(project(c))
        else:
            keep[(c - 3) // 2] = project(c)

    def block(c):
        pl.when(core >= 0)(lambda: place(c))

    block(0)
    pl.semaphore_wait(barrier, len(partners) + core + z)
    for i in range(first):
        send_far(i)
    for k in range(1, nz):
        @pl.when(z - k >= 0)
        def _(k=k):
            pl.semaphore_signal(in_z, inc=1, device_id=peer(0, nz - k), device_id_type=MESH)

    block(1)
    for i in range(first, half):
        send_far(i)
    block(2)
    send_raw(0)
    first_queries()
    block(3)
    combine(0)
    for i in range(1, early):
        send_raw(i)
        combine(i)
    block(4)
    for i in range(early, half):
        send_raw(i)
        combine(i)
    second_queries()
    block(5)

    @pl.when(z + 1 < nz)
    def _():
        pl.semaphore_wait(in_z, nz - 1 - z)

    for i in range(half):
        total = reduce_x(i)

    third_queries()
    for k in (k for pair in offsets for k in pair if k > 0):
        drain(z_in.at[k - 1], z_recv.at[k - 1])
        total += decode(z_in[k - 1])

    own_len.wait()
    live = (lax.broadcasted_iota(jnp.int32, (tokens, 2 * rank), 0) < len_ref[t]).astype(F32)
    lane = lax.broadcasted_iota(jnp.int32, (tokens, 2 * rank), 1)
    both = jnp.where(lane < rank, pltpu.roll(total, rank, 1), total)
    a_high, a_low = split(total * live)
    b_high, b_low = split(both)

    def outer(left_side, right_side):
        return lax.dot_general(left_side, right_side, (((0,), (0,)), ((), ())), preferred_element_type=F32)

    small[...] = (outer(a_high, b_high) + (outer(a_high, b_low) + outer(a_low, b_high)))[0:rank]
    pairs = rank // 2
    lane_half = lax.broadcasted_iota(jnp.int32, (pairs, 2 * rank), 1)
    example = jnp.where(lane_half < rank, small[pl.ds(0, pairs, stride=2), :], small[pl.ds(1, pairs, stride=2), :])
    exall[t] = example.astype(BF16)

    others = [(dx, dz) for dx in range(NX) for dz in range(nz) if (dx, dz) != (0, 0)]
    others.sort(key=lambda step: -(hops(step[0], NX) + hops(step[1], nz)))
    for dx, dz in others:
        send(exall.at[t], exall.at[t], ex_send, ex_recv, peer(dx, dz))
    count = exall.shape[0]

    own_q.wait()
    last_queries()
    rows = qall.shape[1]
    for k in range(0, nd, 2):
        qflat[k * rows:(k + 2) * rows, :] = jnp.concatenate([qall[k], qall[k + 1]], axis=0)

    drain(exall.at[0:count - 1], ex_recv)

    exwide[...] = exall[...].reshape(count * pairs, 2 * rank).astype(F32)
    flat = jnp.concatenate([exwide[pl.ds(r, count, stride=pairs), :] for r in range(pairs)], axis=1)
    out_ref[...] = lax.dot_general(
        flat.astype(BF16), qflat[...], (((1,), (1,)), ((), ())), preferred_element_type=F32
    )

    drain(sent, x_send)
    drain(z_out, z_send)
    drain(qall.at[0:nd - 1], q_send)
    drain(exall.at[0:count - 1], ex_send)


def solution(mesh):
    nt, nd = mesh.shape["tensor"], mesh.shape["dp"]
    nz = nt // NX
    half = nz // 2

    def body(inputs, out_grads, proj_in, proj_out, lengths, queries):
        seqs, tokens, feats = inputs.shape
        grads = out_grads.shape[2]
        rank = proj_in.shape[1]
        lanes = 2 * rank
        block = (tokens, lanes)
        dma = pltpu.SemaphoreType.DMA
        return pl.pallas_call(
            functools.partial(kernel, nz, nd),
            out_shape=pltpu.VMEM((seqs, nd * queries.shape[0]), F32),
            in_specs=[pl.BlockSpec(memory_space=pltpu.HBM)] * 6,
            out_specs=pl.BlockSpec(memory_space=pltpu.VMEM),
            scratch_shapes=[
                pltpu.VMEM((seqs, tokens, feats + grads), BF16),
                pltpu.VMEM((lanes, feats + grads), BF16),
                pltpu.VMEM((feats + grads, lanes), BF16),
                pltpu.SMEM(lengths.shape, jnp.int32),
                pltpu.VMEM((3, half, 2) + block, BF16),
                pltpu.VMEM((2, half, 2) + block, F32),
                pltpu.VMEM((half, 2) + block, BF16),
                pltpu.VMEM((half, 2, 2) + block, BF16),
                pltpu.VMEM((nz - 1,) + block, BF16),
                pltpu.VMEM((nz - 1,) + block, BF16),
                pltpu.VMEM((nd,) + queries.shape, BF16),
                pltpu.VMEM((nd * queries.shape[0], queries.shape[1]), BF16),
                pltpu.VMEM((seqs, rank // 2, lanes), BF16),
                pltpu.VMEM((seqs * rank // 2, lanes), F32),
                pltpu.VMEM((rank, lanes), F32),
                dma((6,)),
            ] + [dma] * 3 + [pltpu.SemaphoreType.REGULAR] + [dma] * 4 + [dma((half, 2)), dma((half,)), dma((nz - 1,))] + [dma, dma((2, nd // 2))],
            compiler_params=pltpu.CompilerParams(
                collective_id=0, has_side_effects=True, vmem_limit_bytes=60 * 1024 * 1024
            ),
        )(*(
            pltpu.with_memory_space_constraint(operand, pltpu.HBM)
            for operand in (inputs, out_grads, proj_in.T, proj_out.T, lengths, queries)
        ))

    return jax.shard_map(
        body,
        mesh=mesh,
        in_specs=(
            P("dp", None, "tensor"),
            P("dp", None, "tensor"),
            P("tensor", None),
            P("tensor", None),
            P("dp"),
            P(("tensor", "dp"), None),
        ),
        out_specs=P("dp", "tensor"),
        check_vma=False,
    )
```

```python
import functools

import jax
import jax.numpy as jnp
from jax import lax
from jax.experimental import pallas as pl
from jax.experimental.pallas import tpu as pltpu
from jax.sharding import PartitionSpec as P

MESH = pl.DeviceIdType.MESH
F32 = jnp.float32
BF16 = jnp.bfloat16
NX = 4


SCALE = 2.0**50


def encode(value):
    scaled = value * SCALE
    return (scaled * jnp.abs(scaled)).astype(BF16)


def decode(code):
    wide = code.astype(F32)
    root = jnp.sqrt(jnp.abs(wide)) * (1.0 / SCALE)
    return jnp.where(wide < 0, -root, root)


def split(value):
    high = value.astype(BF16)
    return high, (value - high.astype(F32)).astype(BF16)


def hops(steps, size):
    return min(steps, size - steps)


def kernel(
    nz, nd,
    x_hbm, g_hbm, wi_hbm, wo_hbm, len_hbm, q_hbm, out_ref,
    acts, wt, w, len_ref, sent, keep, chain_in, final_in, z_out, z_in, qall, qflat, exall, exwide, small,
    load_sem, w_sem, len_sem, own_q_sem, in_z, x_send, z_send, q_send, ex_send, chain_recv, final_recv, z_recv, ex_recv, q_recv,
):
    half = nz // 2
    tokens, rank = x_hbm.shape[1], wi_hbm.shape[0]
    feats = x_hbm.shape[2]
    t = lax.axis_index("tensor")
    d = lax.axis_index("dp")
    x, z = t // nz, t % nz
    x_right, x_left, x_far = (x + 1) % NX, (x + NX - 1) % NX, (x + 2) % NX

    def peer(dx, dz):
        return {"tensor": ((x + dx) % NX) * nz + (z + dz) % nz, "dp": d}

    right, left = peer(1, 0), peer(NX - 1, 0)
    core, y, ny = d % 2, d // 2, nd // 2

    def peer_y(dy, side):
        return {"tensor": t, "dp": ((y + dy) % ny) * 2 + side}

    near_y = sorted({1, ny - 1} - {0}) if ny > 1 else []
    far_y = [k for k in range(1, ny) if k not in near_y]
    barrier = pltpu.get_barrier_semaphore()
    partners = [right, left]
    partners += [peer_y(k, core) for k in near_y]
    for partner in partners:
        pl.semaphore_signal(barrier, inc=1, device_id=partner, device_id_type=MESH)

    @pl.when(core == 0)
    def _():
        pl.semaphore_signal(barrier, inc=1, device_id=peer_y(0, 1), device_id_type=MESH)

    for k in range(1, nz):
        @pl.when(z + k < nz)
        def _(k=k):
            pl.semaphore_signal(barrier, inc=1, device_id=peer(0, k), device_id_type=MESH)

    offsets = [(half + i, half - 1 - i) for i in range(half)]
    chunks = [[], [], [], [], [], []]
    early = (half + 1) // 2
    first = max(half // 4, 1)
    for i, (even, odd) in enumerate(offsets):
        ze, zo = (z + even) % nz, (z + odd) % nz
        chunks[0 if i < first else 1] += [(x_far, ze), (x_far, zo)]
        chunks[2 if i < early else 4] += [(x_right, zo), (x_left, ze)]
        chunks[3] += [(x_right, ze), (x_left, zo)]
        chunks[5] += [(x, ze), (x, zo)]

    starts = [0]
    for owners in chunks:
        starts.append(starts[-1] + len(owners))

    def load(c):
        for k, (xd, zd) in enumerate(chunks[c]):
            s, slot = xd * nz + zd, starts[c] + k
            pltpu.make_async_copy(x_hbm.at[s], acts.at[slot, :, 0:feats], load_sem.at[c]).start()
            pltpu.make_async_copy(g_hbm.at[s], acts.at[slot, :, feats:], load_sem.at[c]).start()

    own_q = pltpu.make_async_copy(q_hbm, qall.at[d], own_q_sem)
    own_len = pltpu.make_async_copy(len_hbm, len_ref, len_sem)
    wt[...] = jnp.zeros_like(wt)
    pltpu.make_async_copy(wi_hbm, wt.at[0:rank, 0:feats], w_sem).start()
    pltpu.make_async_copy(wo_hbm, wt.at[rank:2 * rank, feats:], w_sem).start()
    load(0)

    def drain(ref, sem):
        pltpu.make_async_copy(ref, ref, sem).wait()

    drain(wt.at[0:rank], w_sem)
    for c in range(1, len(chunks)):
        load(c)
    own_q.start()
    own_len.start()
    w[...] = wt[...].T

    def project(c):
        count = starts[c + 1] - starts[c]
        block = acts.at[starts[c]:starts[c + 1]]
        drain(block, load_sem.at[c])
        total = jnp.dot(
            block[:, :, 0:feats].reshape(count * tokens, feats), w[0:feats, :], preferred_element_type=F32
        )
        total += jnp.dot(
            block[:, :, feats:].reshape(count * tokens, block.shape[2] - feats), w[feats:, :], preferred_element_type=F32
        )
        return total.reshape(count // 2, 2, tokens, 2 * rank)

    def send(src, dst, send_sem, recv_sem, device):
        pltpu.make_async_remote_copy(
            src_ref=src, dst_ref=dst, send_sem=send_sem, recv_sem=recv_sem, device_id=device, device_id_type=MESH
        ).start()

    def send_far(i):
        for side, device in enumerate((right, left)):
            send(sent.at[0, i, side], chain_in.at[i, side], x_send, chain_recv.at[i, side], device)

    def send_raw(i):
        send(sent.at[1, i, 0], final_in.at[i, 1, 0], x_send, final_recv.at[i], right)
        send(sent.at[1, i, 1], final_in.at[i, 0, 1], x_send, final_recv.at[i], left)

    def combine(i):
        for side, device in enumerate((right, left)):
            drain(chain_in.at[i, side], chain_recv.at[i, side])
            sent[2, i, side] = encode(keep[0, i, side] + decode(chain_in[i, side]))
            send(sent.at[2, i, side], final_in.at[i, side, side], x_send, final_recv.at[i], device)

    def reduce_x(i):
        drain(final_in.at[i], final_recv.at[i])
        for parity, k in enumerate(offsets[i]):
            total = keep[1, i, parity] + (decode(final_in[i, parity, 0]) + decode(final_in[i, parity, 1]))
            if k == 0:
                return total
            z_out[k - 1] = encode(total)
            send(z_out.at[k - 1], z_in.at[k - 1], z_send, z_recv.at[k - 1], peer(0, k))

    def send_query(k, side):
        send(q_hbm, qall.at[d], q_send, q_recv.at[(core + side) % 2, k], peer_y(k, side))

    def take_query(k, side):
        drain(qall.at[0], q_recv.at[(core + side) % 2, k])

    def on(side):
        return pl.when(core == side)

    def first_queries():
        for k in near_y:
            send_query(k, core)
        on(1)(lambda: send_query(0, 0))

    def second_queries():
        for k in near_y:
            take_query(k, core)
        for k in far_y:
            send_query(k, core)

        @on(1)
        def _():
            for k in near_y:
                send_query(k, 0)

    def third_queries():
        for k in far_y:
            take_query(k, core)

        @on(1)
        def _():
            for k in far_y:
                send_query(k, 0)

        @on(0)
        def _():
            for k in [0] + near_y:
                take_query(k, 1)
                send_query((ny - k) % ny, 1)

    def last_queries():
        @on(0)
        def _():
            for k in far_y:
                take_query(k, 1)
                send_query((ny - k) % ny, 1)

        @on(1)
        def _():
            for k in [0] + near_y + far_y:
                take_query(k, 0)

    def place(c):
        if c == 0:
            sent[0, 0:first] = encode(project(c))
        elif c == 1:
            sent[0, first:] = encode(project(c))
        elif c == 2:
            sent[1, 0:early] = encode(project(c))
        elif c == 4:
            sent[1, early:] = encode(project(c))
        else:
            keep[(c - 3) // 2] = project(c)

    def block(c):
        pl.when(core >= 0)(lambda: place(c))

    block(0)
    pl.semaphore_wait(barrier, len(partners) + core + z)
    for i in range(first):
        send_far(i)
    for k in range(1, nz):
        @pl.when(z - k >= 0)
        def _(k=k):
            pl.semaphore_signal(in_z, inc=1, device_id=peer(0, nz - k), device_id_type=MESH)

    block(1)
    for i in range(first, half):
        send_far(i)
    block(2)
    send_raw(0)
    first_queries()
    block(3)
    combine(0)
    for i in range(1, early):
        send_raw(i)
        combine(i)
    block(4)
    for i in range(early, half):
        send_raw(i)
        combine(i)
    second_queries()
    block(5)

    @pl.when(z + 1 < nz)
    def _():
        pl.semaphore_wait(in_z, nz - 1 - z)

    for i in range(half):
        total = reduce_x(i)

    third_queries()
    for k in (k for pair in offsets for k in pair if k > 0):
        drain(z_in.at[k - 1], z_recv.at[k - 1])
        total += decode(z_in[k - 1])

    own_len.wait()
    live = (lax.broadcasted_iota(jnp.int32, (tokens, 2 * rank), 0) < len_ref[t]).astype(F32)
    lane = lax.broadcasted_iota(jnp.int32, (tokens, 2 * rank), 1)
    both = jnp.where(lane < rank, pltpu.roll(total, rank, 1), total)
    a_high, a_low = split(total * live)
    b_high, b_low = split(both)

    small[...] = lax.dot_general(
        jnp.concatenate([a_high, a_high, a_low], axis=0),
        jnp.concatenate([b_high, b_low, b_high], axis=0),
        (((0,), (0,)), ((), ())),
        preferred_element_type=F32,
    )[0:rank]
    pairs = rank // 2
    lane_half = lax.broadcasted_iota(jnp.int32, (pairs, 2 * rank), 1)
    example = jnp.where(lane_half < rank, small[pl.ds(0, pairs, stride=2), :], small[pl.ds(1, pairs, stride=2), :])
    exall[t] = example.astype(BF16)

    others = [(dx, dz) for dx in range(NX) for dz in range(nz) if (dx, dz) != (0, 0)]
    others.sort(key=lambda step: -(hops(step[0], NX) + hops(step[1], nz)))
    for dx, dz in others:
        send(exall.at[t], exall.at[t], ex_send, ex_recv, peer(dx, dz * (1 - core) + (nz - dz) * core))
    count = exall.shape[0]

    own_q.wait()
    last_queries()
    rows = qall.shape[1]
    for k in range(0, nd, 2):
        qflat[k * rows:(k + 2) * rows, :] = jnp.concatenate([qall[k], qall[k + 1]], axis=0)

    drain(exall.at[0:count - 1], ex_recv)

    exwide[...] = exall[...].reshape(count * pairs, 2 * rank).astype(F32)
    flat = jnp.concatenate([exwide[pl.ds(r, count, stride=pairs), :] for r in range(pairs)], axis=1)
    out_ref[...] = lax.dot_general(
        flat.astype(BF16), qflat[...], (((1,), (1,)), ((), ())), preferred_element_type=F32
    )

    drain(sent, x_send)
    drain(z_out, z_send)
    drain(qall.at[0:nd - 1], q_send)
    drain(exall.at[0:count - 1], ex_send)


def solution(mesh):
    nt, nd = mesh.shape["tensor"], mesh.shape["dp"]
    nz = nt // NX
    half = nz // 2

    def body(inputs, out_grads, proj_in, proj_out, lengths, queries):
        seqs, tokens, feats = inputs.shape
        grads = out_grads.shape[2]
        rank = proj_in.shape[1]
        lanes = 2 * rank
        block = (tokens, lanes)
        dma = pltpu.SemaphoreType.DMA
        return pl.pallas_call(
            functools.partial(kernel, nz, nd),
            out_shape=pltpu.VMEM((seqs, nd * queries.shape[0]), F32),
            in_specs=[pl.BlockSpec(memory_space=pltpu.HBM)] * 6,
            out_specs=pl.BlockSpec(memory_space=pltpu.VMEM),
            scratch_shapes=[
                pltpu.VMEM((seqs, tokens, feats + grads), BF16),
                pltpu.VMEM((lanes, feats + grads), BF16),
                pltpu.VMEM((feats + grads, lanes), BF16),
                pltpu.SMEM(lengths.shape, jnp.int32),
                pltpu.VMEM((3, half, 2) + block, BF16),
                pltpu.VMEM((2, half, 2) + block, F32),
                pltpu.VMEM((half, 2) + block, BF16),
                pltpu.VMEM((half, 2, 2) + block, BF16),
                pltpu.VMEM((nz - 1,) + block, BF16),
                pltpu.VMEM((nz - 1,) + block, BF16),
                pltpu.VMEM((nd,) + queries.shape, BF16),
                pltpu.VMEM((nd * queries.shape[0], queries.shape[1]), BF16),
                pltpu.VMEM((seqs, rank // 2, lanes), BF16),
                pltpu.VMEM((seqs * rank // 2, lanes), F32),
                pltpu.VMEM((rank, lanes), F32),
                dma((6,)),
            ] + [dma] * 3 + [pltpu.SemaphoreType.REGULAR] + [dma] * 4 + [dma((half, 2)), dma((half,)), dma((nz - 1,))] + [dma, dma((2, nd // 2))],
            compiler_params=pltpu.CompilerParams(
                collective_id=0, has_side_effects=True, vmem_limit_bytes=60 * 1024 * 1024
            ),
        )(*(
            pltpu.with_memory_space_constraint(operand, pltpu.HBM)
            for operand in (inputs, out_grads, proj_in.T, proj_out.T, lengths, queries)
        ))

    return jax.shard_map(
        body,
        mesh=mesh,
        in_specs=(
            P("dp", None, "tensor"),
            P("dp", None, "tensor"),
            P("tensor", None),
            P("tensor", None),
            P("dp"),
            P(("tensor", "dp"), None),
        ),
        out_specs=P("dp", "tensor"),
        check_vma=False,
    )
```
